512 devices in a mesh: ctx: 64 (over z, x_lo, core), head: 8 (over y, x_hi).
Axes of the slice: x: 4 (x_hi: 2, x_lo: 2; x = x_hi * 2 + x_lo), y: 4, z: 16, core: 2. Of those that a mesh axis runs over, the one named last changes fastest.
Arguments:
- queries: bfloat16 [16384, 8192], P(('ctx', 'head')), may hold values from -8 to 8
- kv_cache: bfloat16 [2, 131072, 1024], P(None, 'ctx', 'head'), may hold values from -8 to 8
- anchor_src: int32 [64], P('ctx'), may hold values from 0 to 63, as said below
- stretch_pos: int32 [64], P('ctx'), may hold values from 0 to 1792, as said below
Outputs:
- attended: bfloat16 [16384, 8192], P(('ctx', 'head'))
The draws below stay inside these ranges and needn't reach their ends.
Inputs may be any that keep to these rules, and one draw needn't show every extreme that they name: Documents are runs of whole blocks: anchor_src[b] is the first block of block b's document, never after b, the same for all blocks of one document, anchor_src[0] = 0; a document covers 1 to 8 blocks and some document covers exactly 8 blocks. `stretch_pos`: A multiple of 256; some block has the largest value and some block has 0.
All inputs are finite; a program needn't handle non-finite values.
Results may differ from the reference program's by a relative error of at most 0.0055.
Values may be sent and summed in bfloat16 or wider, within the bound.
No kernel may reach another device: no remote copies, remote signals or barrier semaphores. Data moves between devices by JAX's collectives and lax.ppermute only.
A program may use at most 64 MiB of HBM per device.

```python
import math
import jax
import jax.numpy as jnp
from jax import lax

QUERY_HEAD_COUNT = 64
KEY_HEADS = 8
HEAD_SIZE = 128
BLOCK_QUERIES = 256
CACHE_SLOTS = 2048
ANCHOR_SLOTS = 512
SPAN = 8
N_CTX = 64


def draw_queries(key, part):
    key = jax.random.fold_in(key, 7)
    row_total = N_CTX * BLOCK_QUERIES
    value_rows = jax.random.truncated_normal(key, -6.0, 6.0, (row_total, QUERY_HEAD_COUNT * HEAD_SIZE), jnp.float32)
    return value_rows.astype(jnp.bfloat16)


def draw_kv_cache(key, part):
    key = jax.random.fold_in(key, 1)
    row_total = N_CTX * CACHE_SLOTS
    value_rows = jax.random.truncated_normal(key, -6.0, 6.0, (2, row_total, KEY_HEADS * HEAD_SIZE), jnp.float32)
    return value_rows.astype(jnp.bfloat16)


def draw_anchor_src(key, part):
    key = jax.random.fold_in(key, 3)
    lengths = jax.random.randint(jax.random.fold_in(key, 1), (N_CTX,), 1, SPAN + 1)
    starts = jnp.cumsum(lengths) - lengths
    blocks = jnp.arange(N_CTX, dtype=jnp.int32)
    is_start = jnp.any(starts[None, :] == blocks[:, None], axis=1)
    offset = jax.random.randint(jax.random.fold_in(key, 2), (), 0, N_CTX - SPAN)
    inside = (blocks > offset) & (blocks < offset + SPAN)
    is_start = is_start & jnp.logical_not(inside) | (blocks == offset) | (blocks == offset + SPAN) | (blocks == N_CTX - 1)
    return lax.cummax(jnp.where(is_start, blocks, 0), axis=0).astype(jnp.int32)


def draw_stretch_pos(key, part):
    key = jax.random.fold_in(key, 5)
    offsets = jax.random.randint(jax.random.fold_in(key, 1), (N_CTX,), 0, CACHE_SLOTS // BLOCK_QUERIES) * BLOCK_QUERIES
    chosen = jax.random.randint(jax.random.fold_in(key, 2), (), 0, N_CTX)
    second = (chosen + 1 + jax.random.randint(jax.random.fold_in(key, 3), (), 0, N_CTX - 1)) % N_CTX
    offsets = offsets.at[chosen].set(CACHE_SLOTS - BLOCK_QUERIES).at[second].set(0)
    return offsets.astype(jnp.int32)


def setup_inputs(seed: int = 0) -> dict:
    splits = jax.random.split(jax.random.key(seed), 5)
    return {
        "queries": draw_queries(jax.random.fold_in(splits[4], 71), 0),
        "kv_cache": draw_kv_cache(jax.random.fold_in(splits[4], 71), 0),
        "anchor_src": draw_anchor_src(jax.random.fold_in(splits[4], 71), 0),
        "stretch_pos": draw_stretch_pos(jax.random.fold_in(splits[4], 71), 0),
    }


masked_score = -1e+30

def reference(queries, kv_cache, anchor_src, stretch_pos):
    heads_per_group = QUERY_HEAD_COUNT // KEY_HEADS
    scale_factor = 1.0 / math.sqrt(HEAD_SIZE)

    def single_block(block_index):
        query_lines = lax.dynamic_slice_in_dim(queries, block_index * BLOCK_QUERIES, BLOCK_QUERIES, 0)
        query_lines = query_lines.astype(jnp.float32).reshape(BLOCK_QUERIES, KEY_HEADS, heads_per_group, HEAD_SIZE)
        local_kv = lax.dynamic_slice_in_dim(kv_cache, block_index * CACHE_SLOTS, CACHE_SLOTS, 1)
        source = anchor_src[block_index]
        anchor_kv = lax.dynamic_slice_in_dim(kv_cache, source * CACHE_SLOTS, ANCHOR_SLOTS, 1)
        combined_keys = jnp.concatenate([anchor_kv, local_kv], axis=1).astype(jnp.float32)
        combined_keys = combined_keys.reshape(2, ANCHOR_SLOTS + CACHE_SLOTS, KEY_HEADS, HEAD_SIZE)
        scores = jnp.einsum('rhgd,nhd->rhgn', query_lines, combined_keys[0]) * scale_factor
        position = stretch_pos[block_index] + jnp.arange(BLOCK_QUERIES, dtype=jnp.int32)
        local_ok = jnp.arange(CACHE_SLOTS, dtype=jnp.int32)[None, :] <= position[:, None]
        anchor_ok = jnp.broadcast_to(source != block_index, (BLOCK_QUERIES, ANCHOR_SLOTS))
        allowed = jnp.concatenate([anchor_ok, local_ok], axis=1)[:, None, None, :]
        scores = jnp.where(allowed, scores, masked_score)
        peak = lax.optimization_barrier(jnp.max(scores, axis=-1, keepdims=True))
        expo = jnp.where(allowed, jnp.exp(scores - peak), 0.0)
        total = lax.optimization_barrier(jnp.sum(expo, axis=-1))
        weights = lax.optimization_barrier(expo.astype(jnp.bfloat16)).astype(jnp.float32)
        mixed = jnp.einsum('rhgn,nhd->rhgd', weights, combined_keys[1]) / total[..., None]
        return mixed.reshape(BLOCK_QUERIES, QUERY_HEAD_COUNT * HEAD_SIZE).astype(jnp.bfloat16)
    stacked = lax.map(single_block, jnp.arange(N_CTX, dtype=jnp.int32))
    return stacked.reshape(N_CTX * BLOCK_QUERIES, QUERY_HEAD_COUNT * HEAD_SIZE)
```

```python
import functools
import math

import jax
import jax.numpy as jnp
from jax import lax
from jax.experimental import pallas as pl
from jax.experimental.pallas import tpu as pltpu
from jax.sharding import PartitionSpec as P

QUERY_HEAD_COUNT = 64
KEY_HEADS = 8
HEAD_SIZE = 128
GROUP = QUERY_HEAD_COUNT // KEY_HEADS
BLOCK_QUERIES = 256
CACHE_SLOTS = 2048
ANCHOR_SLOTS = 512
SPAN = 8
TILE = 256
LOCAL_TILES = CACHE_SLOTS // TILE
ANCHOR_TILES = ANCHOR_SLOTS // TILE

masked_score = -1e30
EXP2_SCALE = math.log2(math.e) / math.sqrt(HEAD_SIZE)

contract_last = (((1,), (1,)), ((), ()))


def scaled_parts(q):
    wide = q.astype(jnp.float32) * EXP2_SCALE
    high = wide.astype(jnp.bfloat16)
    low = (wide - high.astype(jnp.float32)).astype(jnp.bfloat16)
    return jnp.concatenate([high, low], axis=1)


def attend_kernel(scalars, q_ref, kv_ref, anchor_ref, out_ref, keys, vals, scores):
    full_tiles = scalars[0]
    has_anchor = scalars[1]
    tiles = ANCHOR_TILES + LOCAL_TILES
    for part, first, count in ((anchor_ref, 0, ANCHOR_SLOTS), (kv_ref, ANCHOR_SLOTS, CACHE_SLOTS)):
        keys[pl.ds(first, count), 0:HEAD_SIZE] = part[0]
        keys[pl.ds(first, count), HEAD_SIZE:] = part[0]
        vals[pl.ds(first, count), 0:HEAD_SIZE] = part[1]
        vals[pl.ds(first, count), HEAD_SIZE:] = jnp.ones((count, HEAD_SIZE), jnp.bfloat16)
    row = lax.broadcasted_iota(jnp.int32, (BLOCK_QUERIES, TILE), 0)
    col = lax.broadcasted_iota(jnp.int32, (BLOCK_QUERIES, TILE), 1)
    triangle = col <= row

    def score(q, tile):
        return lax.dot_general(q, keys[pl.ds(tile * TILE, TILE), :], contract_last,
                               preferred_element_type=jnp.float32)

    def finish(g, mixed):
        ratio = mixed[:, :HEAD_SIZE] / mixed[:, HEAD_SIZE:]
        out_ref[:, pl.ds(g * HEAD_SIZE, HEAD_SIZE)] = ratio.astype(jnp.bfloat16)

    def q_of(g):
        return scaled_parts(q_ref[:, pl.ds(pl.multiple_of(g * HEAD_SIZE, HEAD_SIZE), HEAD_SIZE)])

    whole = jnp.logical_and(full_tiles == LOCAL_TILES - 1, has_anchor == 1)

    @pl.when(whole)
    def _():
        def two_heads(pair, carry):
            peaks = []
            for half in range(2):
                q = q_of(pair * 2 + half)
                peak = None
                for tile in range(tiles):
                    s = score(q, tile)
                    if tile == tiles - 1:
                        s = jnp.where(triangle, s, masked_score)
                    scores[half, :, tile * TILE:(tile + 1) * TILE] = s
                    peak = s if peak is None else jnp.maximum(peak, s)
                peaks.append(jnp.max(peak, axis=1, keepdims=True))
            for half in range(2):
                mixed = None
                for tile in range(tiles):
                    s = scores[half, :, tile * TILE:(tile + 1) * TILE]
                    p = jnp.exp2(s - peaks[half]).astype(jnp.bfloat16)
                    part = jnp.dot(p, vals[tile * TILE:(tile + 1) * TILE, :], preferred_element_type=jnp.float32)
                    mixed = part if mixed is None else mixed + part
                finish(pl.multiple_of(pair * 2 + half, 1), mixed)
            return carry

        lax.fori_loop(0, GROUP // 2, two_heads, 0)

    @pl.when(jnp.logical_not(whole))
    def _():
        begin = jnp.where(has_anchor == 1, 0, ANCHOR_TILES)
        last = ANCHOR_TILES + full_tiles

        def one_head(g, carry):
            q = q_of(g)

            def pass_one(tile, peak):
                s = score(q, tile)
                scores[0, :, pl.ds(pl.multiple_of(tile * TILE, TILE), TILE)] = s
                return jnp.maximum(peak, s)

            s = jnp.where(triangle, score(q, last), masked_score)
            scores[0, :, pl.ds(pl.multiple_of(last * TILE, TILE), TILE)] = s
            peak = lax.fori_loop(begin, last, pass_one, s)
            peak = jnp.max(peak, axis=1, keepdims=True)

            def pass_two(tile, mixed):
                s = scores[0, :, pl.ds(pl.multiple_of(tile * TILE, TILE), TILE)]
                p = jnp.exp2(s - peak).astype(jnp.bfloat16)
                return mixed + jnp.dot(p, vals[pl.ds(pl.multiple_of(tile * TILE, TILE), TILE), :],
                                       preferred_element_type=jnp.float32)

            mixed = lax.fori_loop(begin, last + 1, pass_two,
                                  jnp.zeros((BLOCK_QUERIES, 2 * HEAD_SIZE), jnp.float32))
            finish(g, mixed)
            return carry

        lax.fori_loop(0, GROUP, one_head, 0)


def attend(scalars, q, kv, anchor):
    total = ANCHOR_SLOTS + CACHE_SLOTS
    flops = 4 * BLOCK_QUERIES * GROUP * total * HEAD_SIZE
    return pl.pallas_call(
        attend_kernel,
        out_shape=jax.ShapeDtypeStruct(q.shape, jnp.bfloat16),
        in_specs=[pl.BlockSpec(memory_space=pltpu.SMEM)] + [pl.BlockSpec(memory_space=pltpu.VMEM)] * 3,
        out_specs=pl.BlockSpec(memory_space=pltpu.VMEM),
        scratch_shapes=[
            pltpu.VMEM((total, 2 * HEAD_SIZE), jnp.bfloat16),
            pltpu.VMEM((total, 2 * HEAD_SIZE), jnp.bfloat16),
            pltpu.VMEM((2, BLOCK_QUERIES, total), jnp.float32),
        ],
        compiler_params=pltpu.CompilerParams(vmem_limit_bytes=40 * 2**20),
        cost_estimate=pl.CostEstimate(flops=flops, bytes_accessed=2 * 2**20, transcendentals=flops // 512),
        name="attend",
    )(scalars, q, kv, anchor)


def body(queries, kv_cache, anchor_src, stretch_pos):
    block = lax.axis_index("ctx").astype(jnp.int32)
    blocks = lax.axis_size("ctx")
    place = block - anchor_src[0]
    held = kv_cache[:, :ANCHOR_SLOTS, :]
    shift = SPAN // 2
    while shift:
        moved = lax.ppermute(held, "ctx", [(b, b + shift) for b in range(blocks - shift)])
        held = jnp.where((place & shift) != 0, moved, held)
        shift //= 2
    q = lax.all_to_all(queries, "head", split_axis=1, concat_axis=0, tiled=True)
    scalars = jnp.stack([stretch_pos[0] // TILE, (place > 0).astype(jnp.int32)])
    result = attend(scalars, q, kv_cache, held)
    return lax.all_to_all(result, "head", split_axis=0, concat_axis=1, tiled=True)


def solution(mesh):
    in_specs = (P(("ctx", "head"), None), P(None, "ctx", "head"), P("ctx"), P("ctx"))
    out_specs = P(("ctx", "head"), None)
    return jax.shard_map(body, mesh=mesh, in_specs=in_specs, out_specs=out_specs, check_vma=False)
```

```python
import functools
import math

import jax
import jax.numpy as jnp
from jax import lax
from jax.experimental import pallas as pl
from jax.experimental.pallas import tpu as pltpu
from jax.sharding import PartitionSpec as P

QUERY_HEAD_COUNT = 64
KEY_HEADS = 8
HEAD_SIZE = 128
GROUP = QUERY_HEAD_COUNT // KEY_HEADS
BLOCK_QUERIES = 256
CACHE_SLOTS = 2048
ANCHOR_SLOTS = 512
SPAN = 8
TILE = 256
LOCAL_TILES = CACHE_SLOTS // TILE

masked_score = -1e30
EXP2_SCALE = math.log2(math.e) / math.sqrt(HEAD_SIZE)


def scaled_parts(q):
    wide = q.astype(jnp.float32) * EXP2_SCALE
    high = wide.astype(jnp.bfloat16)
    low = (wide - high.astype(jnp.float32)).astype(jnp.bfloat16)
    return jnp.concatenate([high, low], axis=1)


def widen(part_ref, keys, vals, count):
    flipped = part_ref[0].astype(jnp.float32).T.astype(jnp.bfloat16)
    keys[0:HEAD_SIZE, :] = flipped
    keys[HEAD_SIZE:, :] = flipped
    vals[:, 0:HEAD_SIZE] = part_ref[1]
    vals[:, HEAD_SIZE:] = jnp.ones((count, HEAD_SIZE), jnp.bfloat16)


def q_parts(q_ref, g):
    return scaled_parts(q_ref[:, pl.ds(pl.multiple_of(g * HEAD_SIZE, HEAD_SIZE), HEAD_SIZE)])


def fold(s):
    return jnp.maximum(s[:, :HEAD_SIZE], s[:, HEAD_SIZE:])


def local_kernel(scalars, q_ref, kv_ref, state_ref, peak_ref, keys, vals, scores, weights):
    widen(kv_ref, keys, vals, CACHE_SLOTS)
    full_tiles = scalars[0]
    row = lax.broadcasted_iota(jnp.int32, (BLOCK_QUERIES, TILE), 0)
    col = lax.broadcasted_iota(jnp.int32, (BLOCK_QUERIES, TILE), 1)
    slant = col - row

    def variant(tiles, masked):
        span = tiles * TILE

        def first_half(g, slot):
            q = q_parts(q_ref, g)
            peak = None
            for tile in range(tiles):
                at = slice(tile * TILE, (tile + 1) * TILE)
                s = jnp.dot(q, keys[:, at], preferred_element_type=jnp.float32)
                if tile >= masked:
                    s = jnp.where(slant <= (full_tiles - tile) * TILE, s, masked_score)
                scores[slot, :, at] = s
                peak = fold(s) if peak is None else jnp.maximum(peak, fold(s))
            return jnp.max(peak, axis=1, keepdims=True)

        def second_half(g, slot, peak):
            for tile in range(tiles):
                at = slice(tile * TILE, (tile + 1) * TILE)
                weights[slot, :, at] = jnp.exp2(scores[slot, :, at] - peak).astype(jnp.bfloat16)
            state_ref[g] = jnp.dot(weights[slot, :, 0:span], vals[0:span, :], preferred_element_type=jnp.float32)
            peak_ref[g] = jnp.broadcast_to(peak, (BLOCK_QUERIES, HEAD_SIZE))

        def two_heads(pair, peak):
            g = pair * 2
            next_peak = first_half(g + 1, 1)
            second_half(g, 0, peak)
            peak = first_half(jnp.minimum(g + 2, GROUP - 1), 0)
            second_half(g + 1, 1, next_peak)
            return peak

        lax.fori_loop(0, GROUP // 2, two_heads, first_half(0, 0))

    @pl.when(full_tiles == LOCAL_TILES - 1)
    def _():
        variant(LOCAL_TILES, LOCAL_TILES - 1)

    @pl.when(full_tiles < LOCAL_TILES - 1)
    def _():
        variant(LOCAL_TILES - 1, 0)


def anchor_kernel(scalars, q_ref, anchor_ref, state_ref, peak_ref, out_ref, keys, vals):
    widen(anchor_ref, keys, vals, ANCHOR_SLOTS)
    has_anchor = scalars[1] > 0

    def one_head(g):
        s = jnp.dot(q_parts(q_ref, g), keys[...], preferred_element_type=jnp.float32)
        s = jnp.where(has_anchor, s, masked_score)
        old = peak_ref[g]
        peak = jnp.maximum(fold(s[:, :TILE]), fold(s[:, TILE:]))
        peak = jnp.maximum(jnp.max(peak, axis=1, keepdims=True), old[:, :1])
        weights = jnp.exp2(s - peak).astype(jnp.bfloat16)
        mixed = jnp.dot(weights, vals[...], preferred_element_type=jnp.float32)
        mixed = mixed + state_ref[g] * jnp.exp2(old[:, :1] - peak)
        ratio = mixed[:, :HEAD_SIZE] / mixed[:, HEAD_SIZE:]
        out_ref[:, pl.ds(pl.multiple_of(g * HEAD_SIZE, HEAD_SIZE), HEAD_SIZE)] = ratio.astype(jnp.bfloat16)

    def two_heads(pair, carry):
        one_head(pair * 2)
        one_head(pair * 2 + 1)
        return carry

    lax.fori_loop(0, GROUP // 2, two_heads, 0)


def cost(keys):
    flops = 4 * BLOCK_QUERIES * GROUP * keys * HEAD_SIZE
    return pl.CostEstimate(flops=flops, bytes_accessed=2 * 2**20, transcendentals=flops // 512)


smem = pl.BlockSpec(memory_space=pltpu.SMEM)
vmem = pl.BlockSpec(memory_space=pltpu.VMEM)


def attend_local(scalars, q, kv):
    return pl.pallas_call(
        local_kernel,
        out_shape=(
            jax.ShapeDtypeStruct((GROUP, BLOCK_QUERIES, 2 * HEAD_SIZE), jnp.float32),
            jax.ShapeDtypeStruct((GROUP, BLOCK_QUERIES, HEAD_SIZE), jnp.float32),
        ),
        in_specs=[smem, vmem, vmem],
        out_specs=(vmem, vmem),
        scratch_shapes=[
            pltpu.VMEM((2 * HEAD_SIZE, CACHE_SLOTS), jnp.bfloat16),
            pltpu.VMEM((CACHE_SLOTS, 2 * HEAD_SIZE), jnp.bfloat16),
            pltpu.VMEM((2, BLOCK_QUERIES, CACHE_SLOTS), jnp.float32),
            pltpu.VMEM((2, BLOCK_QUERIES, CACHE_SLOTS), jnp.bfloat16),
        ],
        compiler_params=pltpu.CompilerParams(vmem_limit_bytes=40 * 2**20),
        cost_estimate=cost(CACHE_SLOTS),
        name="attend_local",
    )(scalars, q, kv)


def attend_anchor(scalars, q, anchor, state, peak):
    return pl.pallas_call(
        anchor_kernel,
        out_shape=jax.ShapeDtypeStruct(q.shape, jnp.bfloat16),
        in_specs=[smem] + [vmem] * 4,
        out_specs=vmem,
        scratch_shapes=[
            pltpu.VMEM((2 * HEAD_SIZE, ANCHOR_SLOTS), jnp.bfloat16),
            pltpu.VMEM((ANCHOR_SLOTS, 2 * HEAD_SIZE), jnp.bfloat16),
        ],
        compiler_params=pltpu.CompilerParams(vmem_limit_bytes=40 * 2**20),
        cost_estimate=cost(ANCHOR_SLOTS),
        name="attend_anchor",
    )(scalars, q, anchor, state, peak)


def body(queries, kv_cache, anchor_src, stretch_pos):
    block = lax.axis_index("ctx").astype(jnp.int32)
    blocks = lax.axis_size("ctx")
    place = block - anchor_src[0]
    scalars = jnp.stack([stretch_pos[0] // TILE, place])
    q = lax.all_to_all(queries, "head", split_axis=1, concat_axis=0, tiled=True)
    held = kv_cache[:, :ANCHOR_SLOTS, :]
    shift = SPAN // 2
    while shift:
        moved = lax.ppermute(held, "ctx", [(b, b + shift) for b in range(blocks - shift)])
        held = jnp.where((place & shift) != 0, moved, held)
        shift //= 2
    state, peak = attend_local(scalars, q, kv_cache)
    result = attend_anchor(scalars, q, held, state, peak)
    return lax.all_to_all(result, "head", split_axis=0, concat_axis=1, tiled=True)


def solution(mesh):
    in_specs = (P(("ctx", "head"), None), P(None, "ctx", "head"), P("ctx"), P("ctx"))
    out_specs = P(("ctx", "head"), None)
    return jax.shard_map(body, mesh=mesh, in_specs=in_specs, out_specs=out_specs, check_vma=False)
```

```python
import functools
import math

import jax
import jax.numpy as jnp
from jax import lax
from jax.experimental import pallas as pl
from jax.experimental.pallas import tpu as pltpu
from jax.sharding import PartitionSpec as P

QUERY_HEAD_COUNT = 64
KEY_HEADS = 8
HEAD_SIZE = 128
GROUP = QUERY_HEAD_COUNT // KEY_HEADS
BLOCK_QUERIES = 256
CACHE_SLOTS = 2048
ANCHOR_SLOTS = 512
SPAN = 8
TILE = 256
FIRST_HEADS = 3
LOCAL_TILES = CACHE_SLOTS // TILE

masked_score = -1e30
EXP2_SCALE = math.log2(math.e) / math.sqrt(HEAD_SIZE)


def scaled_parts(q):
    wide = q.astype(jnp.float32) * EXP2_SCALE
    high = wide.astype(jnp.bfloat16)
    low = (wide - high.astype(jnp.float32)).astype(jnp.bfloat16)
    return jnp.concatenate([high, low], axis=1)


def prepare_kernel(queries, kv, outgoing, anchor, sems):
    heads, _, width = outgoing.shape
    copies = [pltpu.make_async_copy(kv.at[:, pl.ds(0, ANCHOR_SLOTS), :], anchor, sems.at[heads])]
    for h in range(heads):
        copies.append(pltpu.make_async_copy(queries.at[:, pl.ds(h * width, width)], outgoing.at[h], sems.at[h]))
    for copy in copies:
        copy.start()
    for copy in copies:
        copy.wait()


def widen_into(part_ref, keys, vals):
    flipped = part_ref[0].astype(jnp.float32).T.astype(jnp.bfloat16)
    keys[0:HEAD_SIZE, :] = flipped
    keys[HEAD_SIZE:, :] = flipped
    vals[:, 0:HEAD_SIZE] = part_ref[1]
    vals[:, HEAD_SIZE:] = jnp.ones(part_ref.shape[1:], jnp.bfloat16)


def fold(s):
    return jnp.maximum(s[:, :HEAD_SIZE], s[:, HEAD_SIZE:])


def local_kernel(first, scalars, q_ref, keys, vals, state_ref, peak_ref, parts_ref, scores, weights):
    heads = state_ref.shape[0]
    full_tiles = scalars[0]
    row = lax.broadcasted_iota(jnp.int32, (BLOCK_QUERIES, TILE), 0)
    col = lax.broadcasted_iota(jnp.int32, (BLOCK_QUERIES, TILE), 1)
    slant = col - row

    def variant(tiles, masked):
        span = tiles * TILE

        def first_half(g, slot):
            q = scaled_parts(q_ref[:, (first + g) * HEAD_SIZE:(first + g + 1) * HEAD_SIZE])
            parts_ref[g] = q
            peak = None
            for tile in range(tiles):
                at = slice(tile * TILE, (tile + 1) * TILE)
                s = jnp.dot(q, keys[:, at], preferred_element_type=jnp.float32)
                if tile >= masked:
                    s = jnp.where(slant <= (full_tiles - tile) * TILE, s, masked_score)
                scores[slot, :, at] = s
                peak = fold(s) if peak is None else jnp.maximum(peak, fold(s))
            return jnp.max(peak, axis=1, keepdims=True)

        def second_half(g, slot, peak):
            for tile in range(tiles):
                at = slice(tile * TILE, (tile + 1) * TILE)
                weights[slot, :, at] = jnp.exp2(scores[slot, :, at] - peak).astype(jnp.bfloat16)
            state_ref[g] = jnp.dot(weights[slot, :, 0:span], vals[0:span, :], preferred_element_type=jnp.float32)
            peak_ref[g] = jnp.broadcast_to(peak, (BLOCK_QUERIES, HEAD_SIZE))

        peak = first_half(0, 0)
        for g in range(heads):
            next_peak = first_half(g + 1, (g + 1) % 2) if g + 1 < heads else None
            second_half(g, g % 2, peak)
            peak = next_peak

    @pl.when(full_tiles == LOCAL_TILES - 1)
    def _():
        variant(LOCAL_TILES, LOCAL_TILES - 1)

    @pl.when(full_tiles < LOCAL_TILES - 1)
    def _():
        variant(LOCAL_TILES - 1, 0)


def anchor_kernel(scalars, anchor_ref, *refs):
    *inputs, out_ref, keys, vals, scores = refs
    widen_into(anchor_ref, keys, vals)
    has_anchor = scalars[1] > 0
    heads = []
    for state_ref, peak_ref, parts_ref in zip(inputs[0::3], inputs[1::3], inputs[2::3]):
        heads += [(state_ref.at[g], peak_ref.at[g], parts_ref.at[g]) for g in range(state_ref.shape[0])]
    peaks = []
    for g, (_, old, parts) in enumerate(heads):
        s = jnp.dot(parts[...], keys[...], preferred_element_type=jnp.float32)
        s = jnp.where(has_anchor, s, masked_score)
        scores[g] = s
        peak = jnp.maximum(fold(s[:, :TILE]), fold(s[:, TILE:]))
        peaks.append(jnp.maximum(jnp.max(peak, axis=1, keepdims=True), old[:, :1]))
    for g, (state, old, _) in enumerate(heads):
        weights = jnp.exp2(scores[g] - peaks[g]).astype(jnp.bfloat16)
        mixed = jnp.dot(weights, vals[...], preferred_element_type=jnp.float32)
        mixed = mixed + state[...] * jnp.exp2(old[:, :1] - peaks[g])
        ratio = mixed[:, :HEAD_SIZE] / mixed[:, HEAD_SIZE:]
        out_ref[:, g * HEAD_SIZE:(g + 1) * HEAD_SIZE] = ratio.astype(jnp.bfloat16)


def cost(heads, keys):
    flops = 4 * BLOCK_QUERIES * heads * keys * HEAD_SIZE
    return pl.CostEstimate(flops=flops, bytes_accessed=2 * 2**20, transcendentals=flops // 512)


smem = pl.BlockSpec(memory_space=pltpu.SMEM)
vmem = pl.BlockSpec(memory_space=pltpu.VMEM)
hbm = pl.BlockSpec(memory_space=pltpu.HBM)
params = pltpu.CompilerParams(vmem_limit_bytes=40 * 2**20)


def wide_shapes(count):
    return (jax.ShapeDtypeStruct((2 * HEAD_SIZE, count), jnp.bfloat16),
            jax.ShapeDtypeStruct((count, 2 * HEAD_SIZE), jnp.bfloat16))


def prepare(queries, kv):
    rows, width = queries.shape
    return pl.pallas_call(
        prepare_kernel,
        out_shape=(
            jax.ShapeDtypeStruct((KEY_HEADS, rows, width // KEY_HEADS), jnp.bfloat16),
            jax.ShapeDtypeStruct((2, ANCHOR_SLOTS, HEAD_SIZE), jnp.bfloat16),
        ),
        in_specs=[hbm, hbm],
        out_specs=(hbm, hbm),
        scratch_shapes=[pltpu.SemaphoreType.DMA((KEY_HEADS + 1,))],
        compiler_params=pltpu.CompilerParams(vmem_limit_bytes=60 * 2**20),
        name="prepare",
    )(queries, kv)


def widen(kv):
    return pl.pallas_call(
        widen_into,
        out_shape=wide_shapes(CACHE_SLOTS),
        in_specs=[vmem],
        out_specs=(vmem, vmem),
        compiler_params=params,
        name="widen",
    )(kv)


def attend_local(first, heads, scalars, q, keys, vals):
    return pl.pallas_call(
        functools.partial(local_kernel, first),
        out_shape=(
            jax.ShapeDtypeStruct((heads, BLOCK_QUERIES, 2 * HEAD_SIZE), jnp.float32),
            jax.ShapeDtypeStruct((heads, BLOCK_QUERIES, HEAD_SIZE), jnp.float32),
            jax.ShapeDtypeStruct((heads, BLOCK_QUERIES, 2 * HEAD_SIZE), jnp.bfloat16),
        ),
        in_specs=[smem, vmem, vmem, vmem],
        out_specs=(vmem, vmem, vmem),
        scratch_shapes=[
            pltpu.VMEM((2, BLOCK_QUERIES, CACHE_SLOTS), jnp.float32),
            pltpu.VMEM((2, BLOCK_QUERIES, CACHE_SLOTS), jnp.bfloat16),
        ],
        compiler_params=params,
        cost_estimate=cost(heads, CACHE_SLOTS),
        name="attend_local",
    )(scalars, q, keys, vals)


def attend_anchor(scalars, anchor, *states):
    return pl.pallas_call(
        anchor_kernel,
        out_shape=jax.ShapeDtypeStruct((BLOCK_QUERIES, GROUP * HEAD_SIZE), jnp.bfloat16),
        in_specs=[smem] + [vmem] * (1 + len(states)),
        out_specs=vmem,
        scratch_shapes=[
            *(pltpu.VMEM(wide.shape, wide.dtype) for wide in wide_shapes(ANCHOR_SLOTS)),
            pltpu.VMEM((GROUP, BLOCK_QUERIES, ANCHOR_SLOTS), jnp.float32),
        ],
        compiler_params=params,
        cost_estimate=cost(GROUP, ANCHOR_SLOTS),
        name="attend_anchor",
    )(scalars, anchor, *states)


def body(queries, kv_cache, anchor_src, stretch_pos):
    block = lax.axis_index("ctx").astype(jnp.int32)
    blocks = lax.axis_size("ctx")
    place = block - anchor_src[0]
    scalars = jnp.stack([stretch_pos[0] // TILE, place])
    outgoing, held = prepare(queries, kv_cache)
    q = lax.all_to_all(outgoing, "head", split_axis=0, concat_axis=0, tiled=True)
    q = q.reshape(BLOCK_QUERIES, GROUP * HEAD_SIZE)

    def from_earlier(held, shift):
        moved = lax.ppermute(held, "ctx", [(b, b + shift) for b in range(blocks - shift)])
        return jnp.where((place & shift) != 0, moved, held)

    held = from_earlier(held, 4)
    held, kv = lax.optimization_barrier((held, kv_cache))
    held = from_earlier(held, 2)
    keys, vals = widen(kv)
    early = attend_local(0, FIRST_HEADS, scalars, q, keys, vals)
    held, q, *early = lax.optimization_barrier((held, q, *early))
    held = from_earlier(held, 1)
    late = attend_local(FIRST_HEADS, GROUP - FIRST_HEADS, scalars, q, keys, vals)
    result = attend_anchor(scalars, held, *early, *late)
    return lax.all_to_all(result, "head", split_axis=0, concat_axis=1, tiled=True)


def solution(mesh):
    in_specs = (P(("ctx", "head"), None), P(None, "ctx", "head"), P("ctx"), P("ctx"))
    out_specs = P(("ctx", "head"), None)
    return jax.shard_map(body, mesh=mesh, in_specs=in_specs, out_specs=out_specs, check_vma=False)
```

```python
import functools
import math

import jax
import jax.numpy as jnp
from jax import lax
from jax.experimental import pallas as pl
from jax.experimental.pallas import tpu as pltpu
from jax.sharding import PartitionSpec as P

QUERY_HEAD_COUNT = 64
KEY_HEADS = 8
HEAD_SIZE = 128
GROUP = QUERY_HEAD_COUNT // KEY_HEADS
BLOCK_QUERIES = 256
CACHE_SLOTS = 2048
ANCHOR_SLOTS = 512
SPAN = 8
TILE = 256
FIRST_HEADS = 3
LOCAL_TILES = CACHE_SLOTS // TILE

masked_score = -1e30
EXP2_SCALE = math.log2(math.e) / math.sqrt(HEAD_SIZE)


def scaled_parts(q):
    wide = q.astype(jnp.float32) * EXP2_SCALE
    high = wide.astype(jnp.bfloat16)
    low = (wide - high.astype(jnp.float32)).astype(jnp.bfloat16)
    return jnp.concatenate([high, low], axis=1)


def prepare_kernel(queries, kv, outgoing, anchor, sems):
    heads, _, width = outgoing.shape
    copies = [pltpu.make_async_copy(kv.at[:, pl.ds(0, ANCHOR_SLOTS), :], anchor, sems.at[heads])]
    for h in range(heads):
        copies.append(pltpu.make_async_copy(queries.at[:, pl.ds(h * width, width)], outgoing.at[h], sems.at[h]))
    for copy in copies:
        copy.start()
    for copy in copies:
        copy.wait()


def widen_into(part_ref, keys, vals):
    flipped = part_ref[0].astype(jnp.float32).T.astype(jnp.bfloat16)
    keys[0:HEAD_SIZE, :] = flipped
    keys[HEAD_SIZE:, :] = flipped
    vals[:, 0:HEAD_SIZE] = part_ref[1]
    vals[:, HEAD_SIZE:] = jnp.ones(part_ref.shape[1:], jnp.bfloat16)


def fold(s):
    return jnp.maximum(s[:, :HEAD_SIZE], s[:, HEAD_SIZE:])


def local_kernel(first, scalars, q_ref, keys, vals, state_ref, peak_ref, parts_ref, scores, weights):
    heads = state_ref.shape[0]
    full_tiles = scalars[0]
    row = lax.broadcasted_iota(jnp.int32, (BLOCK_QUERIES, TILE), 0)
    col = lax.broadcasted_iota(jnp.int32, (BLOCK_QUERIES, TILE), 1)
    slant = col - row

    def variant(tiles, masked):
        span = tiles * TILE

        def first_half(g, slot):
            q = scaled_parts(q_ref[:, (first + g) * HEAD_SIZE:(first + g + 1) * HEAD_SIZE])
            parts_ref[g] = q
            peak = None
            for tile in range(tiles):
                at = slice(tile * TILE, (tile + 1) * TILE)
                s = jnp.dot(q, keys[:, at], preferred_element_type=jnp.float32)
                if tile >= masked:
                    s = jnp.where(slant <= (full_tiles - tile) * TILE, s, masked_score)
                scores[slot, :, at] = s
                peak = fold(s) if peak is None else jnp.maximum(peak, fold(s))
            return jnp.max(peak, axis=1, keepdims=True)

        def second_half(g, slot, peak):
            for tile in range(tiles):
                at = slice(tile * TILE, (tile + 1) * TILE)
                weights[slot, :, at] = jnp.exp2(scores[slot, :, at] - peak).astype(jnp.bfloat16)
            state_ref[g] = jnp.dot(weights[slot, :, 0:span], vals[0:span, :], preferred_element_type=jnp.float32)
            peak_ref[g] = jnp.broadcast_to(peak, (BLOCK_QUERIES, HEAD_SIZE))

        peak = first_half(0, 0)
        for g in range(heads):
            next_peak = first_half(g + 1, (g + 1) % 2) if g + 1 < heads else None
            second_half(g, g % 2, peak)
            peak = next_peak

    @pl.when(full_tiles == LOCAL_TILES - 1)
    def _():
        variant(LOCAL_TILES, LOCAL_TILES - 1)

    @pl.when(full_tiles < LOCAL_TILES - 1)
    def _():
        variant(LOCAL_TILES - 1, 0)


def anchor_kernel(scalars, anchor_ref, *refs):
    *inputs, out_ref, keys, vals, scores, weights = refs
    widen_into(anchor_ref, keys, vals)
    has_anchor = scalars[1] > 0
    heads = []
    for state_ref, peak_ref, parts_ref in zip(inputs[0::3], inputs[1::3], inputs[2::3]):
        heads += [(state_ref.at[g], peak_ref.at[g], parts_ref.at[g]) for g in range(state_ref.shape[0])]
    columns = [slice(c, c + HEAD_SIZE) for c in range(0, ANCHOR_SLOTS, HEAD_SIZE)]
    peaks = []
    for g, (_, old, parts) in enumerate(heads):
        s = jnp.dot(parts[...], keys[...], preferred_element_type=jnp.float32)
        s = jnp.where(has_anchor, s, masked_score)
        scores[g] = s
        peak = jnp.maximum(fold(s[:, :TILE]), fold(s[:, TILE:]))
        peaks.append(jnp.maximum(jnp.max(peak, axis=1, keepdims=True), old[...]))
    for g, (state, old, _) in enumerate(heads):
        for at in columns:
            weights[g % 2, :, at] = jnp.exp2(scores[g, :, at] - peaks[g]).astype(jnp.bfloat16)
        mixed = jnp.dot(weights[g % 2], vals[...], preferred_element_type=jnp.float32)
        factor = jnp.exp2(old[...] - peaks[g])
        top = mixed[:, :HEAD_SIZE] + state[:, :HEAD_SIZE] * factor
        bottom = mixed[:, HEAD_SIZE:] + state[:, HEAD_SIZE:] * factor
        out_ref[:, g * HEAD_SIZE:(g + 1) * HEAD_SIZE] = (top / bottom).astype(jnp.bfloat16)


def cost(heads, keys):
    flops = 4 * BLOCK_QUERIES * heads * keys * HEAD_SIZE
    return pl.CostEstimate(flops=flops, bytes_accessed=2 * 2**20, transcendentals=flops // 512)


smem = pl.BlockSpec(memory_space=pltpu.SMEM)
vmem = pl.BlockSpec(memory_space=pltpu.VMEM)
anywhere = pl.BlockSpec(memory_space=pl.ANY)
params = pltpu.CompilerParams(vmem_limit_bytes=24 * 2**20)


def wide_shapes(count):
    return (jax.ShapeDtypeStruct((2 * HEAD_SIZE, count), jnp.bfloat16),
            jax.ShapeDtypeStruct((count, 2 * HEAD_SIZE), jnp.bfloat16))


def prepare(queries, kv):
    rows, width = queries.shape
    return pl.pallas_call(
        prepare_kernel,
        out_shape=(
            jax.ShapeDtypeStruct((KEY_HEADS, rows, width // KEY_HEADS), jnp.bfloat16),
            jax.ShapeDtypeStruct((2, ANCHOR_SLOTS, HEAD_SIZE), jnp.bfloat16),
        ),
        in_specs=[anywhere, anywhere],
        out_specs=(vmem, vmem),
        scratch_shapes=[pltpu.SemaphoreType.DMA((KEY_HEADS + 1,))],
        compiler_params=params,
        name="prepare",
    )(queries, kv)


def widen(kv):
    return pl.pallas_call(
        widen_into,
        out_shape=wide_shapes(CACHE_SLOTS),
        in_specs=[vmem],
        out_specs=(vmem, vmem),
        compiler_params=params,
        name="widen",
    )(kv)


def attend_local(first, heads, scalars, q, keys, vals):
    return pl.pallas_call(
        functools.partial(local_kernel, first),
        out_shape=(
            jax.ShapeDtypeStruct((heads, BLOCK_QUERIES, 2 * HEAD_SIZE), jnp.float32),
            jax.ShapeDtypeStruct((heads, BLOCK_QUERIES, HEAD_SIZE), jnp.float32),
            jax.ShapeDtypeStruct((heads, BLOCK_QUERIES, 2 * HEAD_SIZE), jnp.bfloat16),
        ),
        in_specs=[smem, vmem, vmem, vmem],
        out_specs=(vmem, vmem, vmem),
        scratch_shapes=[
            pltpu.VMEM((2, BLOCK_QUERIES, CACHE_SLOTS), jnp.float32),
            pltpu.VMEM((2, BLOCK_QUERIES, CACHE_SLOTS), jnp.bfloat16),
        ],
        compiler_params=params,
        cost_estimate=cost(heads, CACHE_SLOTS),
        name="attend_local",
    )(scalars, q, keys, vals)


def attend_anchor(scalars, anchor, *states):
    return pl.pallas_call(
        anchor_kernel,
        out_shape=jax.ShapeDtypeStruct((BLOCK_QUERIES, GROUP * HEAD_SIZE), jnp.bfloat16),
        in_specs=[smem] + [vmem] * (1 + len(states)),
        out_specs=vmem,
        scratch_shapes=[
            *(pltpu.VMEM(wide.shape, wide.dtype) for wide in wide_shapes(ANCHOR_SLOTS)),
            pltpu.VMEM((GROUP, BLOCK_QUERIES, ANCHOR_SLOTS), jnp.float32),
            pltpu.VMEM((2, BLOCK_QUERIES, ANCHOR_SLOTS), jnp.bfloat16),
        ],
        compiler_params=params,
        cost_estimate=cost(GROUP, ANCHOR_SLOTS),
        name="attend_anchor",
    )(scalars, anchor, *states)


def body(queries, kv_cache, anchor_src, stretch_pos):
    block = lax.axis_index("ctx").astype(jnp.int32)
    blocks = lax.axis_size("ctx")
    place = block - anchor_src[0]
    scalars = jnp.stack([stretch_pos[0] // TILE, place])
    outgoing, held = prepare(queries, kv_cache)
    q = lax.all_to_all(outgoing, "head", split_axis=0, concat_axis=0, tiled=True)
    q = q.reshape(BLOCK_QUERIES, GROUP * HEAD_SIZE)

    def from_earlier(held, shift):
        moved = lax.ppermute(held, "ctx", [(b, b + shift) for b in range(blocks - shift)])
        return jnp.where((place & shift) != 0, moved, held)

    held = from_earlier(held, 4)
    held, kv = lax.optimization_barrier((held, kv_cache))
    held = from_earlier(held, 2)
    keys, vals = widen(kv)
    early = attend_local(0, FIRST_HEADS, scalars, q, keys, vals)
    held, q, *early = lax.optimization_barrier((held, q, *early))
    held = from_earlier(held, 1)
    late = attend_local(FIRST_HEADS, GROUP - FIRST_HEADS, scalars, q, keys, vals)
    result = attend_anchor(scalars, held, *early, *late)
    return lax.all_to_all(result, "head", split_axis=0, concat_axis=1, tiled=True)


def solution(mesh):
    in_specs = (P(("ctx", "head"), None), P(None, "ctx", "head"), P("ctx"), P("ctx"))
    out_specs = P(("ctx", "head"), None)
    return jax.shard_map(body, mesh=mesh, in_specs=in_specs, out_specs=out_specs, check_vma=False)
```

```python
import functools
import math

import jax
import jax.numpy as jnp
from jax import lax
from jax.experimental import pallas as pl
from jax.experimental.pallas import tpu as pltpu
from jax.sharding import PartitionSpec as P

QUERY_HEAD_COUNT = 64
KEY_HEADS = 8
HEAD_SIZE = 128
GROUP = QUERY_HEAD_COUNT // KEY_HEADS
BLOCK_QUERIES = 256
CACHE_SLOTS = 2048
ANCHOR_SLOTS = 512
SPAN = 8
TILE = 256
FIRST_HEADS = 1
LOCAL_TILES = CACHE_SLOTS // TILE
ANCHOR_TILES = ANCHOR_SLOTS // TILE

masked_score = -1e30
EXP2_SCALE = math.log2(math.e) / math.sqrt(HEAD_SIZE)
SAFE_LOW, SAFE_HIGH = 2.0**-60, 2.0**60


def head_columns(g):
    return slice(g * HEAD_SIZE, (g + 1) * HEAD_SIZE)


def cut_kernel(queries, outgoing):
    pieces, _, width = outgoing.shape
    for h in range(pieces):
        outgoing[h] = queries[:, h * width:(h + 1) * width]


def choose_kernel(shift, scalars, moved, held, out):
    arrived = (scalars[1] & shift) != 0

    @pl.when(arrived)
    def _():
        out[...] = moved[...]

    @pl.when(jnp.logical_not(arrived))
    def _():
        out[...] = held[...]


def widen_into(part_ref, keys, vals):
    keys[...] = part_ref[0].astype(jnp.float32).T.astype(jnp.bfloat16)
    vals[:, 0:HEAD_SIZE] = part_ref[1]
    vals[:, HEAD_SIZE:] = jnp.ones(part_ref.shape[1:], jnp.bfloat16)


def scaled_scores(q, keys):
    return jnp.dot(q, keys, preferred_element_type=jnp.float32) * EXP2_SCALE


def is_safe(low, high):
    return jnp.logical_and(jnp.min(low) > SAFE_LOW, jnp.max(high) < SAFE_HIGH).astype(jnp.int32)


def local_kernel(first, scalars, q_ref, keys, vals, state_ref, peak_ref, safe_ref, scores, weights):
    heads = state_ref.shape[0]
    full_tiles = scalars[0]
    row = lax.broadcasted_iota(jnp.int32, (BLOCK_QUERIES, TILE), 0)
    col = lax.broadcasted_iota(jnp.int32, (BLOCK_QUERIES, TILE), 1)
    slant = col - row

    def tile_of(tile):
        return slice(tile * TILE, (tile + 1) * TILE)

    def unshifted(tiles, masked):
        span = tiles * TILE

        def weigh(g):
            q = q_ref[:, head_columns(first + g)]
            for tile in range(tiles):
                s = scaled_scores(q, keys[:, tile_of(tile)])
                if tile >= masked:
                    s = jnp.where(slant <= (full_tiles - tile) * TILE, s, masked_score)
                weights[g % 2, :, tile_of(tile)] = jnp.exp2(s).astype(jnp.bfloat16)

        low = high = None
        weigh(0)
        for g in range(heads):
            if g + 1 < heads:
                weigh(g + 1)
            mixed = jnp.dot(weights[g % 2, :, 0:span], vals[0:span, :], preferred_element_type=jnp.float32)
            state_ref[g] = mixed
            peak_ref[g] = jnp.zeros(peak_ref.shape[1:], jnp.float32)
            total = mixed[:, HEAD_SIZE:]
            low = total if low is None else jnp.minimum(low, total)
            high = total if high is None else jnp.maximum(high, total)
        safe_ref[0] = is_safe(low, high)

    @pl.when(full_tiles == LOCAL_TILES - 1)
    def _():
        unshifted(LOCAL_TILES, LOCAL_TILES - 1)

    @pl.when(full_tiles < LOCAL_TILES - 1)
    def _():
        unshifted(LOCAL_TILES - 1, 0)

    @pl.when(safe_ref[0] == 0)
    def _():
        def tile_at(tile):
            return pl.ds(pl.multiple_of(tile * TILE, TILE), TILE)

        for g in range(heads):
            q = q_ref[:, head_columns(first + g)]

            def score_tile(tile, peak):
                s = scaled_scores(q, keys[:, tile_at(tile)])
                s = jnp.where(slant <= (full_tiles - tile) * TILE, s, masked_score)
                scores[:, tile_at(tile)] = s
                return jnp.maximum(peak, jnp.max(s, axis=1, keepdims=True))

            peak = lax.fori_loop(0, full_tiles + 1, score_tile,
                                 jnp.full((BLOCK_QUERIES, 1), masked_score, jnp.float32))

            def mix_tile(tile, mixed):
                p = jnp.exp2(scores[:, tile_at(tile)] - peak).astype(jnp.bfloat16)
                return mixed + jnp.dot(p, vals[tile_at(tile), :], preferred_element_type=jnp.float32)

            state_ref[g] = lax.fori_loop(0, full_tiles + 1, mix_tile,
                                         jnp.zeros((BLOCK_QUERIES, 2 * HEAD_SIZE), jnp.float32))
            peak_ref[g] = jnp.broadcast_to(peak, peak_ref.shape[1:])


def anchor_kernel(scalars, early_safe, late_safe, moved, held, q_ref, *refs):
    *inputs, out_ref, anchor, keys, vals, weights, safe_ref = refs
    has_anchor = scalars[1] > 0
    choose_kernel(1, scalars, moved, held, anchor)
    widen_into(anchor, keys, vals)
    heads = []
    for state_ref, peak_ref in zip(inputs[0::2], inputs[1::2]):
        heads += [(state_ref.at[g], peak_ref.at[g]) for g in range(state_ref.shape[0])]

    def score(g):
        s = scaled_scores(q_ref[:, head_columns(g)], keys[...])
        return jnp.where(has_anchor, s, masked_score)

    def mix(g):
        return jnp.dot(weights[g % 2], vals[...], preferred_element_type=jnp.float32)

    def write(g, top, bottom):
        out_ref[:, head_columns(g)] = (top / bottom).astype(jnp.bfloat16)

    def weigh(g):
        weights[g % 2] = jnp.exp2(score(g)).astype(jnp.bfloat16)

    high = None
    weigh(0)
    for g, (state, _) in enumerate(heads):
        if g + 1 < GROUP:
            weigh(g + 1)
        mixed = mix(g) + state[...]
        total = mixed[:, HEAD_SIZE:]
        write(g, mixed[:, :HEAD_SIZE], total)
        high = total if high is None else jnp.maximum(high, total)
    safe_ref[0] = is_safe(jnp.ones_like(high), high) * early_safe[0] * late_safe[0]

    @pl.when(safe_ref[0] == 0)
    def _():
        for g, (state, old) in enumerate(heads):
            s = score(g)
            peak = jnp.maximum(jnp.max(s, axis=1, keepdims=True), old[...])
            for at in range(0, ANCHOR_SLOTS, HEAD_SIZE):
                p = jnp.exp2(s[:, at:at + HEAD_SIZE] - peak)
                weights[g % 2, :, at:at + HEAD_SIZE] = p.astype(jnp.bfloat16)
            mixed = mix(g)
            factor = jnp.exp2(old[...] - peak)
            write(g, mixed[:, :HEAD_SIZE] + state[:, :HEAD_SIZE] * factor,
                  mixed[:, HEAD_SIZE:] + state[:, HEAD_SIZE:] * factor)


def cost(heads, keys):
    flops = 4 * BLOCK_QUERIES * heads * keys * HEAD_SIZE
    return pl.CostEstimate(flops=flops, bytes_accessed=2 * 2**20, transcendentals=flops // 512)


smem = pl.BlockSpec(memory_space=pltpu.SMEM)
vmem = pl.BlockSpec(memory_space=pltpu.VMEM)
small = pltpu.CompilerParams(vmem_limit_bytes=4 * 2**20)
params = pltpu.CompilerParams(vmem_limit_bytes=24 * 2**20)
safe_flag = jax.ShapeDtypeStruct((1,), jnp.int32)


def wide_shapes(count):
    return (jax.ShapeDtypeStruct((HEAD_SIZE, count), jnp.bfloat16),
            jax.ShapeDtypeStruct((count, 2 * HEAD_SIZE), jnp.bfloat16))


def cut(queries):
    rows, width = queries.shape
    return pl.pallas_call(
        cut_kernel,
        out_shape=jax.ShapeDtypeStruct((KEY_HEADS, rows, width // KEY_HEADS), jnp.bfloat16),
        in_specs=[vmem],
        out_specs=vmem,
        compiler_params=small,
        name="cut",
    )(queries)


def choose(shift, scalars, moved, held):
    return pl.pallas_call(
        functools.partial(choose_kernel, shift),
        out_shape=jax.ShapeDtypeStruct(held.shape, held.dtype),
        in_specs=[smem, vmem, vmem],
        out_specs=vmem,
        compiler_params=small,
        name="choose",
    )(scalars, moved, held)


def widen(kv):
    return pl.pallas_call(
        widen_into,
        out_shape=wide_shapes(CACHE_SLOTS),
        in_specs=[vmem],
        out_specs=(vmem, vmem),
        compiler_params=params,
        name="widen",
    )(kv)


def attend_local(first, heads, estimate, scalars, q, keys, vals):
    return pl.pallas_call(
        functools.partial(local_kernel, first),
        out_shape=(
            jax.ShapeDtypeStruct((heads, BLOCK_QUERIES, 2 * HEAD_SIZE), jnp.float32),
            jax.ShapeDtypeStruct((heads, BLOCK_QUERIES, HEAD_SIZE), jnp.float32),
            safe_flag,
        ),
        in_specs=[smem, vmem, vmem, vmem],
        out_specs=(vmem, vmem, smem),
        scratch_shapes=[
            pltpu.VMEM((BLOCK_QUERIES, CACHE_SLOTS), jnp.float32),
            pltpu.VMEM((2, BLOCK_QUERIES, CACHE_SLOTS), jnp.bfloat16),
        ],
        compiler_params=params,
        cost_estimate=estimate,
        name="attend_local",
    )(scalars, q, keys, vals)


def attend_anchor(scalars, moved, held, q, early, late):
    states = (*early[:2], *late[:2])
    return pl.pallas_call(
        anchor_kernel,
        out_shape=jax.ShapeDtypeStruct((BLOCK_QUERIES, GROUP * HEAD_SIZE), jnp.bfloat16),
        in_specs=[smem] * 3 + [vmem] * (3 + len(states)),
        out_specs=vmem,
        scratch_shapes=[
            pltpu.VMEM(held.shape, held.dtype),
            *(pltpu.VMEM(wide.shape, wide.dtype) for wide in wide_shapes(ANCHOR_SLOTS)),
            pltpu.VMEM((2, BLOCK_QUERIES, ANCHOR_SLOTS), jnp.bfloat16),
            pltpu.SMEM((1,), jnp.int32),
        ],
        compiler_params=params,
        cost_estimate=cost(GROUP, ANCHOR_SLOTS),
        name="attend_anchor",
    )(scalars, early[2], late[2], moved, held, q, *states)


def body(queries, kv_cache, anchor_src, stretch_pos):
    block = lax.axis_index("ctx").astype(jnp.int32)
    blocks = lax.axis_size("ctx")
    scalars = jnp.stack([stretch_pos[0] // TILE, block - anchor_src[0]])
    held, scalars = lax.optimization_barrier((kv_cache[:, :ANCHOR_SLOTS, :], scalars))

    def from_earlier(held, shift):
        return lax.ppermute(held, "ctx", [(b, b + shift) for b in range(blocks - shift)])

    moved = from_earlier(held, 4)
    q = lax.all_to_all(cut(queries), "head", split_axis=0, concat_axis=0, tiled=True)
    q = q.reshape(BLOCK_QUERIES, GROUP * HEAD_SIZE)
    held = choose(4, scalars, moved, held)
    held, kv = lax.optimization_barrier((held, kv_cache))
    moved = from_earlier(held, 2)
    keys, vals = widen(kv)
    early = attend_local(0, FIRST_HEADS, cost(GROUP, CACHE_SLOTS), scalars, q, keys, vals)
    moved, q, *early = lax.optimization_barrier((moved, q, *early))
    held = choose(2, scalars, moved, held)
    moved = from_earlier(held, 1)
    rest = GROUP - FIRST_HEADS
    late = attend_local(FIRST_HEADS, rest, cost(rest, CACHE_SLOTS), scalars, q, keys, vals)
    result = attend_anchor(scalars, moved, held, q, early, late)
    return lax.all_to_all(result, "head", split_axis=0, concat_axis=1, tiled=True)


def solution(mesh):
    in_specs = (P(("ctx", "head"), None), P(None, "ctx", "head"), P("ctx"), P("ctx"))
    out_specs = P(("ctx", "head"), None)
    return jax.shard_map(body, mesh=mesh, in_specs=in_specs, out_specs=out_specs, check_vma=False)
```

```python
import functools
import math

import jax
import jax.numpy as jnp
from jax import lax
from jax.experimental import pallas as pl
from jax.experimental.pallas import tpu as pltpu
from jax.sharding import PartitionSpec as P

QUERY_HEAD_COUNT = 64
KEY_HEADS = 8
HEAD_SIZE = 128
GROUP = QUERY_HEAD_COUNT // KEY_HEADS
BLOCK_QUERIES = 256
CACHE_SLOTS = 2048
ANCHOR_SLOTS = 512
SPAN = 8
TILE = 256
HALF = GROUP // 2
LOCAL_TILES = CACHE_SLOTS // TILE
ANCHOR_TILES = ANCHOR_SLOTS // TILE

masked_score = -1e30
EXP2_SCALE = math.log2(math.e) / math.sqrt(HEAD_SIZE)
SAFE_LOW, SAFE_HIGH = 2.0**-60, 2.0**60


def head_columns(g):
    return slice(g * HEAD_SIZE, (g + 1) * HEAD_SIZE)


def cut_kernel(queries, early, late):
    pieces, _, width = early.shape
    for h in range(pieces):
        early[h] = queries[:, 2 * h * width:(2 * h + 1) * width]
        late[h] = queries[:, (2 * h + 1) * width:(2 * h + 2) * width]


def join_kernel(early, late, out):
    pieces, _, width = early.shape
    for h in range(pieces):
        out[:, 2 * h * width:(2 * h + 1) * width] = early[h]
        out[:, (2 * h + 1) * width:(2 * h + 2) * width] = late[h]


def choose_kernel(shift, scalars, moved, held, out):
    arrived = (scalars[1] & shift) != 0

    @pl.when(arrived)
    def _():
        out[...] = moved[...]

    @pl.when(jnp.logical_not(arrived))
    def _():
        out[...] = held[...]


def widen_into(part_ref, keys, vals):
    keys[...] = part_ref[0].astype(jnp.float32).T.astype(jnp.bfloat16)
    vals[:, 0:HEAD_SIZE] = part_ref[1]
    vals[:, HEAD_SIZE:] = jnp.ones(part_ref.shape[1:], jnp.bfloat16)


def scaled_scores(q, keys):
    return jnp.dot(q, keys, preferred_element_type=jnp.float32) * EXP2_SCALE


def is_safe(low, high):
    return jnp.logical_and(jnp.min(low) > SAFE_LOW, jnp.max(high) < SAFE_HIGH).astype(jnp.int32)


def local_kernel(scalars, q_ref, keys, vals, state_ref, peak_ref, safe_ref, scores, weights):
    heads = state_ref.shape[0]
    full_tiles = scalars[0]
    row = lax.broadcasted_iota(jnp.int32, (BLOCK_QUERIES, TILE), 0)
    col = lax.broadcasted_iota(jnp.int32, (BLOCK_QUERIES, TILE), 1)
    slant = col - row

    def tile_of(tile):
        return slice(tile * TILE, (tile + 1) * TILE)

    def unshifted(tiles, masked):
        span = tiles * TILE

        def weigh(g):
            q = q_ref[:, head_columns(g)]
            for tile in range(tiles):
                s = scaled_scores(q, keys[:, tile_of(tile)])
                if tile >= masked:
                    s = jnp.where(slant <= (full_tiles - tile) * TILE, s, masked_score)
                weights[g % 2, :, tile_of(tile)] = jnp.exp2(s).astype(jnp.bfloat16)

        low = high = None
        weigh(0)
        for g in range(heads):
            if g + 1 < heads:
                weigh(g + 1)
            mixed = jnp.dot(weights[g % 2, :, 0:span], vals[0:span, :], preferred_element_type=jnp.float32)
            state_ref[g] = mixed
            peak_ref[g] = jnp.zeros(peak_ref.shape[1:], jnp.float32)
            total = mixed[:, HEAD_SIZE:]
            low = total if low is None else jnp.minimum(low, total)
            high = total if high is None else jnp.maximum(high, total)
        safe_ref[0] = is_safe(low, high)

    @pl.when(full_tiles == LOCAL_TILES - 1)
    def _():
        unshifted(LOCAL_TILES, LOCAL_TILES - 1)

    @pl.when(full_tiles < LOCAL_TILES - 1)
    def _():
        unshifted(LOCAL_TILES - 1, 0)

    @pl.when(safe_ref[0] == 0)
    def _():
        def tile_at(tile):
            return pl.ds(pl.multiple_of(tile * TILE, TILE), TILE)

        for g in range(heads):
            q = q_ref[:, head_columns(g)]

            def score_tile(tile, peak):
                s = scaled_scores(q, keys[:, tile_at(tile)])
                s = jnp.where(slant <= (full_tiles - tile) * TILE, s, masked_score)
                scores[:, tile_at(tile)] = s
                return jnp.maximum(peak, jnp.max(s, axis=1, keepdims=True))

            peak = lax.fori_loop(0, full_tiles + 1, score_tile,
                                 jnp.full((BLOCK_QUERIES, 1), masked_score, jnp.float32))

            def mix_tile(tile, mixed):
                p = jnp.exp2(scores[:, tile_at(tile)] - peak).astype(jnp.bfloat16)
                return mixed + jnp.dot(p, vals[tile_at(tile), :], preferred_element_type=jnp.float32)

            state_ref[g] = lax.fori_loop(0, full_tiles + 1, mix_tile,
                                         jnp.zeros((BLOCK_QUERIES, 2 * HEAD_SIZE), jnp.float32))
            peak_ref[g] = jnp.broadcast_to(peak, peak_ref.shape[1:])


def anchor_kernel(scalars, safe, moved, held, q_ref, states, peaks, out_ref, anchor, keys, vals, weights, safe_ref):
    heads = states.shape[0]
    has_anchor = scalars[1] > 0
    choose_kernel(1, scalars, moved, held, anchor)
    widen_into(anchor, keys, vals)

    def score(g):
        s = scaled_scores(q_ref[:, head_columns(g)], keys[...])
        return jnp.where(has_anchor, s, masked_score)

    def mix(g):
        return jnp.dot(weights[g], vals[...], preferred_element_type=jnp.float32)

    def write(g, top, bottom):
        out_ref[:, head_columns(g)] = (top / bottom).astype(jnp.bfloat16)

    for g in range(heads):
        weights[g] = jnp.exp2(score(g)).astype(jnp.bfloat16)
    high = None
    for g in range(heads):
        mixed = mix(g) + states[g]
        total = mixed[:, HEAD_SIZE:]
        write(g, mixed[:, :HEAD_SIZE], total)
        high = total if high is None else jnp.maximum(high, total)
    safe_ref[0] = is_safe(jnp.ones_like(high), high) * safe[0]

    @pl.when(safe_ref[0] == 0)
    def _():
        for g in range(heads):
            s = score(g)
            old = peaks[g]
            peak = jnp.maximum(jnp.max(s, axis=1, keepdims=True), old)
            for at in range(0, ANCHOR_SLOTS, HEAD_SIZE):
                p = jnp.exp2(s[:, at:at + HEAD_SIZE] - peak)
                weights[g, :, at:at + HEAD_SIZE] = p.astype(jnp.bfloat16)
            mixed = mix(g)
            factor = jnp.exp2(old - peak)
            write(g, mixed[:, :HEAD_SIZE] + states[g, :, :HEAD_SIZE] * factor,
                  mixed[:, HEAD_SIZE:] + states[g, :, HEAD_SIZE:] * factor)


def cost(heads, keys):
    flops = 4 * BLOCK_QUERIES * heads * keys * HEAD_SIZE
    return pl.CostEstimate(flops=flops, bytes_accessed=2 * 2**20, transcendentals=flops // 512)


smem = pl.BlockSpec(memory_space=pltpu.SMEM)
vmem = pl.BlockSpec(memory_space=pltpu.VMEM)
small = pltpu.CompilerParams(vmem_limit_bytes=4 * 2**20)
params = pltpu.CompilerParams(vmem_limit_bytes=24 * 2**20)
slight = pl.CostEstimate(flops=1000, bytes_accessed=1000, transcendentals=0)
safe_flag = jax.ShapeDtypeStruct((1,), jnp.int32)


def wide_shapes(count):
    return (jax.ShapeDtypeStruct((HEAD_SIZE, count), jnp.bfloat16),
            jax.ShapeDtypeStruct((count, 2 * HEAD_SIZE), jnp.bfloat16))


def cut(queries):
    rows, width = queries.shape
    piece = jax.ShapeDtypeStruct((KEY_HEADS, rows, width // KEY_HEADS // 2), jnp.bfloat16)
    return pl.pallas_call(
        cut_kernel,
        out_shape=(piece, piece),
        in_specs=[vmem],
        out_specs=(vmem, vmem),
        compiler_params=small,
        cost_estimate=slight,
        name="cut",
    )(queries)


def join(early, late):
    pieces, rows, width = early.shape
    return pl.pallas_call(
        join_kernel,
        out_shape=jax.ShapeDtypeStruct((rows, 2 * pieces * width), early.dtype),
        in_specs=[vmem, vmem],
        out_specs=vmem,
        compiler_params=small,
        cost_estimate=slight,
        name="join",
    )(early, late)


def choose(shift, scalars, moved, held):
    return pl.pallas_call(
        functools.partial(choose_kernel, shift),
        out_shape=jax.ShapeDtypeStruct(held.shape, held.dtype),
        in_specs=[smem, vmem, vmem],
        out_specs=vmem,
        compiler_params=small,
        cost_estimate=slight,
        name="choose",
    )(scalars, moved, held)


def widen(kv):
    return pl.pallas_call(
        widen_into,
        out_shape=wide_shapes(CACHE_SLOTS),
        in_specs=[vmem],
        out_specs=(vmem, vmem),
        compiler_params=params,
        cost_estimate=slight,
        name="widen",
    )(kv)


def attend_local(scalars, q, keys, vals):
    return pl.pallas_call(
        local_kernel,
        out_shape=(
            jax.ShapeDtypeStruct((HALF, BLOCK_QUERIES, 2 * HEAD_SIZE), jnp.float32),
            jax.ShapeDtypeStruct((HALF, BLOCK_QUERIES, HEAD_SIZE), jnp.float32),
            safe_flag,
        ),
        in_specs=[smem, vmem, vmem, vmem],
        out_specs=(vmem, vmem, smem),
        scratch_shapes=[
            pltpu.VMEM((BLOCK_QUERIES, CACHE_SLOTS), jnp.float32),
            pltpu.VMEM((2, BLOCK_QUERIES, CACHE_SLOTS), jnp.bfloat16),
        ],
        compiler_params=params,
        cost_estimate=cost(GROUP, CACHE_SLOTS),
        name="attend_local",
    )(scalars, q, keys, vals)


def attend_anchor(scalars, moved, held, q, states, peaks, safe):
    return pl.pallas_call(
        anchor_kernel,
        out_shape=jax.ShapeDtypeStruct(q.shape, jnp.bfloat16),
        in_specs=[smem] * 2 + [vmem] * 5,
        out_specs=vmem,
        scratch_shapes=[
            pltpu.VMEM(held.shape, held.dtype),
            *(pltpu.VMEM(wide.shape, wide.dtype) for wide in wide_shapes(ANCHOR_SLOTS)),
            pltpu.VMEM((HALF, BLOCK_QUERIES, ANCHOR_SLOTS), jnp.bfloat16),
            pltpu.SMEM((1,), jnp.int32),
        ],
        compiler_params=params,
        cost_estimate=cost(GROUP, ANCHOR_SLOTS),
        name="attend_anchor",
    )(scalars, safe, moved, held, q, states, peaks)


def body(queries, kv_cache, anchor_src, stretch_pos):
    block = lax.axis_index("ctx").astype(jnp.int32)
    blocks = lax.axis_size("ctx")
    scalars = jnp.stack([stretch_pos[0] // TILE, block - anchor_src[0]])
    held, scalars, queries = lax.optimization_barrier((kv_cache[:, :ANCHOR_SLOTS, :], scalars, queries))

    def from_earlier(held, shift):
        return lax.ppermute(held, "ctx", [(b, b + shift) for b in range(blocks - shift)])

    def exchange(pieces):
        return lax.all_to_all(pieces, "head", split_axis=0, concat_axis=0, tiled=True)

    def to_block(piece):
        return exchange(piece).reshape(BLOCK_QUERIES, HALF * HEAD_SIZE)

    def to_owner(result):
        return exchange(result.reshape(KEY_HEADS, BLOCK_QUERIES // KEY_HEADS, HALF * HEAD_SIZE))

    moved = from_earlier(held, 4)
    early, late = cut(queries)
    early, late = to_block(early), to_block(late)
    held = choose(4, scalars, moved, held)
    held, kv = lax.optimization_barrier((held, kv_cache))
    moved = from_earlier(held, 2)
    keys, vals = widen(kv)
    early_state = attend_local(scalars, early, keys, vals)
    moved, late, *early_state = lax.optimization_barrier((moved, late, *early_state))
    held = choose(2, scalars, moved, held)
    moved = from_earlier(held, 1)
    late_state = attend_local(scalars, late, keys, vals)
    early = attend_anchor(scalars, moved, held, early, *early_state)
    late = attend_anchor(scalars, moved, held, late, *late_state)
    return join(to_owner(early), to_owner(late))


def solution(mesh):
    in_specs = (P(("ctx", "head"), None), P(None, "ctx", "head"), P("ctx"), P("ctx"))
    out_specs = P(("ctx", "head"), None)
    return jax.shard_map(body, mesh=mesh, in_specs=in_specs, out_specs=out_specs, check_vma=False)
```

```python
import functools
import math

import jax
import jax.numpy as jnp
from jax import lax
from jax.experimental import pallas as pl
from jax.experimental.pallas import tpu as pltpu
from jax.sharding import PartitionSpec as P

QUERY_HEAD_COUNT = 64
KEY_HEADS = 8
HEAD_SIZE = 128
GROUP = QUERY_HEAD_COUNT // KEY_HEADS
BLOCK_QUERIES = 256
CACHE_SLOTS = 2048
ANCHOR_SLOTS = 512
SPAN = 8
TILE = 256
LOCAL_TILES = CACHE_SLOTS // TILE
ANCHOR_TILES = ANCHOR_SLOTS // TILE

masked_score = -1e30
EXP2_SCALE = math.log2(math.e) / math.sqrt(HEAD_SIZE)
SAFE_LOW, SAFE_HIGH = 2.0**-60, 2.0**60


def head_columns(g):
    return slice(g * HEAD_SIZE, (g + 1) * HEAD_SIZE)


def cut_kernel(queries, outgoing):
    pieces, _, width = outgoing.shape
    for h in range(pieces):
        outgoing[h] = queries[:, h * width:(h + 1) * width]


def choose_copy(shift, scalars, near, far, held, out, sem):
    wanted = (scalars[1] & shift) != 0
    upper = (scalars[2] & shift) != 0

    def fetch(condition, source):
        @pl.when(condition)
        def _():
            copy = pltpu.make_async_copy(source, out, sem)
            copy.start()
            copy.wait()

    fetch(jnp.logical_and(wanted, upper), near.at[0])
    fetch(jnp.logical_and(wanted, jnp.logical_not(upper)), far.at[0])
    fetch(jnp.logical_not(wanted), held)


def widen_into(part_ref, keys, vals):
    keys[...] = part_ref[0].astype(jnp.float32).T.astype(jnp.bfloat16)
    vals[:, 0:HEAD_SIZE] = part_ref[1]
    vals[:, HEAD_SIZE:] = jnp.ones(part_ref.shape[1:], jnp.bfloat16)


def scaled_scores(q, keys):
    return jnp.dot(q, keys, preferred_element_type=jnp.float32) * EXP2_SCALE


def is_safe(low, high):
    return jnp.logical_and(jnp.min(low) > SAFE_LOW, jnp.max(high) < SAFE_HIGH).astype(jnp.int32)


def local_kernel(scalars, q_ref, keys, vals, state_ref, peak_ref, safe_ref, scores, weights):
    heads = state_ref.shape[0]
    full_tiles = scalars[0]
    row = lax.broadcasted_iota(jnp.int32, (BLOCK_QUERIES, TILE), 0)
    col = lax.broadcasted_iota(jnp.int32, (BLOCK_QUERIES, TILE), 1)
    slant = col - row

    def tile_of(tile):
        return slice(tile * TILE, (tile + 1) * TILE)

    def unshifted(tiles, masked):
        span = tiles * TILE

        def weigh(g):
            q = q_ref[:, head_columns(g)]
            for tile in range(tiles):
                s = scaled_scores(q, keys[:, tile_of(tile)])
                if tile >= masked:
                    s = jnp.where(slant <= (full_tiles - tile) * TILE, s, masked_score)
                weights[g % 2, :, tile_of(tile)] = jnp.exp2(s).astype(jnp.bfloat16)

        low = high = None
        weigh(0)
        for g in range(heads):
            if g + 1 < heads:
                weigh(g + 1)
            mixed = jnp.dot(weights[g % 2, :, 0:span], vals[0:span, :], preferred_element_type=jnp.float32)
            state_ref[g] = mixed
            peak_ref[g] = jnp.zeros(peak_ref.shape[1:], jnp.float32)
            total = mixed[:, HEAD_SIZE:]
            low = total if low is None else jnp.minimum(low, total)
            high = total if high is None else jnp.maximum(high, total)
        safe_ref[0] = is_safe(low, high)

    @pl.when(full_tiles == LOCAL_TILES - 1)
    def _():
        unshifted(LOCAL_TILES, LOCAL_TILES - 1)

    @pl.when(full_tiles < LOCAL_TILES - 1)
    def _():
        unshifted(LOCAL_TILES - 1, 0)

    @pl.when(safe_ref[0] == 0)
    def _():
        def tile_at(tile):
            return pl.ds(pl.multiple_of(tile * TILE, TILE), TILE)

        for g in range(heads):
            q = q_ref[:, head_columns(g)]

            def score_tile(tile, peak):
                s = scaled_scores(q, keys[:, tile_at(tile)])
                s = jnp.where(slant <= (full_tiles - tile) * TILE, s, masked_score)
                scores[:, tile_at(tile)] = s
                return jnp.maximum(peak, jnp.max(s, axis=1, keepdims=True))

            peak = lax.fori_loop(0, full_tiles + 1, score_tile,
                                 jnp.full((BLOCK_QUERIES, 1), masked_score, jnp.float32))

            def mix_tile(tile, mixed):
                p = jnp.exp2(scores[:, tile_at(tile)] - peak).astype(jnp.bfloat16)
                return mixed + jnp.dot(p, vals[tile_at(tile), :], preferred_element_type=jnp.float32)

            state_ref[g] = lax.fori_loop(0, full_tiles + 1, mix_tile,
                                         jnp.zeros((BLOCK_QUERIES, 2 * HEAD_SIZE), jnp.float32))
            peak_ref[g] = jnp.broadcast_to(peak, peak_ref.shape[1:])


def anchor_kernel(scalars, safe, near, far, held, q_ref, states, peaks, out_ref,
                  anchor, keys, vals, weights, safe_ref, sem):
    heads = states.shape[0]
    has_anchor = scalars[1] > 0
    choose_copy(1, scalars, near, far, held, anchor, sem)
    widen_into(anchor, keys, vals)

    def score(g):
        s = scaled_scores(q_ref[:, head_columns(g)], keys[...])
        return jnp.where(has_anchor, s, masked_score)

    def mix(g):
        return jnp.dot(weights[g], vals[...], preferred_element_type=jnp.float32)

    def write(g, top, bottom):
        out_ref[:, head_columns(g)] = (top / bottom).astype(jnp.bfloat16)

    for g in range(heads):
        weights[g] = jnp.exp2(score(g)).astype(jnp.bfloat16)
    high = None
    for g in range(heads):
        mixed = mix(g) + states[g]
        total = mixed[:, HEAD_SIZE:]
        write(g, mixed[:, :HEAD_SIZE], total)
        high = total if high is None else jnp.maximum(high, total)
    safe_ref[0] = is_safe(jnp.ones_like(high), high) * safe[0]

    @pl.when(safe_ref[0] == 0)
    def _():
        for g in range(heads):
            s = score(g)
            old = peaks[g]
            peak = jnp.maximum(jnp.max(s, axis=1, keepdims=True), old)
            for at in range(0, ANCHOR_SLOTS, HEAD_SIZE):
                p = jnp.exp2(s[:, at:at + HEAD_SIZE] - peak)
                weights[g, :, at:at + HEAD_SIZE] = p.astype(jnp.bfloat16)
            mixed = mix(g)
            factor = jnp.exp2(old - peak)
            write(g, mixed[:, :HEAD_SIZE] + states[g, :, :HEAD_SIZE] * factor,
                  mixed[:, HEAD_SIZE:] + states[g, :, HEAD_SIZE:] * factor)


def cost(heads, keys):
    flops = 4 * BLOCK_QUERIES * heads * keys * HEAD_SIZE
    return pl.CostEstimate(flops=flops, bytes_accessed=2 * 2**20, transcendentals=flops // 512)


smem = pl.BlockSpec(memory_space=pltpu.SMEM)
vmem = pl.BlockSpec(memory_space=pltpu.VMEM)
anywhere = pl.BlockSpec(memory_space=pl.ANY)
small = pltpu.CompilerParams(vmem_limit_bytes=4 * 2**20)
params = pltpu.CompilerParams(vmem_limit_bytes=24 * 2**20)
whole = pltpu.CompilerParams(vmem_limit_bytes=62 * 2**20)
slight = pl.CostEstimate(flops=1000, bytes_accessed=1000, transcendentals=0)
safe_flag = jax.ShapeDtypeStruct((1,), jnp.int32)


def wide_shapes(count):
    return (jax.ShapeDtypeStruct((HEAD_SIZE, count), jnp.bfloat16),
            jax.ShapeDtypeStruct((count, 2 * HEAD_SIZE), jnp.bfloat16))


def cut(queries):
    rows, width = queries.shape
    return pl.pallas_call(
        cut_kernel,
        out_shape=jax.ShapeDtypeStruct((KEY_HEADS, rows, width // KEY_HEADS), jnp.bfloat16),
        in_specs=[vmem],
        out_specs=vmem,
        compiler_params=small,
        cost_estimate=slight,
        name="cut",
    )(queries)


def choose(shift, scalars, near, far, held):
    return pl.pallas_call(
        functools.partial(choose_copy, shift),
        out_shape=jax.ShapeDtypeStruct(held.shape, held.dtype),
        in_specs=[smem, anywhere, anywhere, anywhere],
        out_specs=vmem,
        scratch_shapes=[pltpu.SemaphoreType.DMA(())],
        compiler_params=whole,
        cost_estimate=slight,
        name="choose",
    )(scalars, near, far, held)


def mark_kernel(scalars, q_ref, out):
    for i in range(out.shape[0]):
        out[i] = scalars[i]


def mark(scalars, q):
    return pl.pallas_call(
        mark_kernel,
        out_shape=jax.ShapeDtypeStruct(scalars.shape, scalars.dtype),
        in_specs=[smem, anywhere],
        out_specs=smem,
        compiler_params=small,
        cost_estimate=cost(GROUP, CACHE_SLOTS),
        name="mark",
    )(scalars, q)


def widen(kv):
    return pl.pallas_call(
        widen_into,
        out_shape=wide_shapes(CACHE_SLOTS),
        in_specs=[vmem],
        out_specs=(vmem, vmem),
        compiler_params=params,
        cost_estimate=slight,
        name="widen",
    )(kv)


def attend_local(scalars, q, keys, vals):
    return pl.pallas_call(
        local_kernel,
        out_shape=(
            jax.ShapeDtypeStruct((GROUP, BLOCK_QUERIES, 2 * HEAD_SIZE), jnp.float32),
            jax.ShapeDtypeStruct((GROUP, BLOCK_QUERIES, HEAD_SIZE), jnp.float32),
            safe_flag,
        ),
        in_specs=[smem, vmem, vmem, vmem],
        out_specs=(vmem, vmem, smem),
        scratch_shapes=[
            pltpu.VMEM((BLOCK_QUERIES, CACHE_SLOTS), jnp.float32),
            pltpu.VMEM((2, BLOCK_QUERIES, CACHE_SLOTS), jnp.bfloat16),
        ],
        compiler_params=params,
        cost_estimate=cost(GROUP, CACHE_SLOTS),
        name="attend_local",
    )(scalars, q, keys, vals)


def attend_anchor(scalars, near, far, held, q, states, peaks, safe):
    return pl.pallas_call(
        anchor_kernel,
        out_shape=jax.ShapeDtypeStruct(q.shape, jnp.bfloat16),
        in_specs=[smem] * 2 + [anywhere] * 3 + [vmem] * 3,
        out_specs=vmem,
        scratch_shapes=[
            pltpu.VMEM(held.shape, held.dtype),
            *(pltpu.VMEM(wide.shape, wide.dtype) for wide in wide_shapes(ANCHOR_SLOTS)),
            pltpu.VMEM((GROUP, BLOCK_QUERIES, ANCHOR_SLOTS), jnp.bfloat16),
            pltpu.SMEM((1,), jnp.int32),
            pltpu.SemaphoreType.DMA(()),
        ],
        compiler_params=params,
        cost_estimate=cost(GROUP, ANCHOR_SLOTS),
        name="attend_anchor",
    )(scalars, safe, near, far, held, q, states, peaks)


def body(queries, kv_cache, anchor_src, stretch_pos):
    block = lax.axis_index("ctx").astype(jnp.int32)
    blocks = lax.axis_size("ctx")
    scalars = jnp.stack([stretch_pos[0] // TILE, block - anchor_src[0], block])
    held, scalars = lax.optimization_barrier((kv_cache[:, :ANCHOR_SLOTS, :], scalars))

    def pairs(held, shift):
        gathered = []
        for odd in range(2):
            lower = [b for b in range(blocks) if (b // shift) % 2 == odd]
            groups = [[b, (b + shift) % blocks] for b in lower]
            gathered.append(lax.all_gather(held, "ctx", axis_index_groups=groups))
        return gathered

    near, far = pairs(held, 4)
    q = lax.all_to_all(cut(queries), "head", split_axis=0, concat_axis=0, tiled=True)
    q = q.reshape(BLOCK_QUERIES, GROUP * HEAD_SIZE)
    held = choose(4, scalars, near, far, held)
    near, far = pairs(held, 2)
    held = choose(2, mark(scalars, q), near, far, held)
    near, far = pairs(held, 1)
    keys, vals = widen(kv_cache)
    state = attend_local(scalars, q, keys, vals)
    result = attend_anchor(scalars, near, far, held, q, *state)
    return lax.all_to_all(result, "head", split_axis=0, concat_axis=1, tiled=True)


def solution(mesh):
    in_specs = (P(("ctx", "head"), None), P(None, "ctx", "head"), P("ctx"), P("ctx"))
    out_specs = P(("ctx", "head"), None)
    return jax.shard_map(body, mesh=mesh, in_specs=in_specs, out_specs=out_specs, check_vma=False)
```

```python
import functools
import math

import jax
import jax.numpy as jnp
from jax import lax
from jax.experimental import pallas as pl
from jax.experimental.pallas import tpu as pltpu
from jax.sharding import PartitionSpec as P

QUERY_HEAD_COUNT = 64
KEY_HEADS = 8
HEAD_SIZE = 128
GROUP = QUERY_HEAD_COUNT // KEY_HEADS
BLOCK_QUERIES = 256
CACHE_SLOTS = 2048
ANCHOR_SLOTS = 512
SPAN = 8
TILE = 256
FIRST_HEADS = 3
ROWS = BLOCK_QUERIES // KEY_HEADS
LOCAL_TILES = CACHE_SLOTS // TILE
ANCHOR_TILES = ANCHOR_SLOTS // TILE

masked_score = -1e30
EXP2_SCALE = math.log2(math.e) / math.sqrt(HEAD_SIZE)
SAFE_LOW, SAFE_HIGH = 2.0**-60, 2.0**60


def head_columns(g):
    return slice(g * HEAD_SIZE, (g + 1) * HEAD_SIZE)


def columns_of(mine, k, width):
    return pl.ds(pl.multiple_of((mine ^ k) * width, width), width)


def cut_kernel(scalars, queries, *pieces):
    for k, piece in enumerate(pieces):
        piece[...] = queries[:, columns_of(scalars[2], k, piece.shape[1])]


def join_kernel(scalars, *refs):
    *pieces, out = refs
    for k, piece in enumerate(pieces):
        out[:, columns_of(scalars[2], k, piece.shape[1])] = piece[...]


def stacked(pieces, g):
    return jnp.concatenate([piece[:, head_columns(g)] for piece in pieces], axis=0)


def token_rows(mine, shape):
    row = lax.broadcasted_iota(jnp.int32, shape, 0)
    return ((row // ROWS) ^ mine) * ROWS + row % ROWS


def choose_kernel(shift, scalars, moved, held, out):
    arrived = (scalars[1] & shift) != 0

    @pl.when(arrived)
    def _():
        out[...] = moved[...]

    @pl.when(jnp.logical_not(arrived))
    def _():
        out[...] = held[...]


def widen_into(part_ref, keys, vals):
    keys[...] = part_ref[0].astype(jnp.float32).T.astype(jnp.bfloat16)
    vals[:, 0:HEAD_SIZE] = part_ref[1]
    vals[:, HEAD_SIZE:] = jnp.ones(part_ref.shape[1:], jnp.bfloat16)


def scaled_scores(q, keys):
    return jnp.dot(q, keys, preferred_element_type=jnp.float32) * EXP2_SCALE


def is_safe(low, high):
    return jnp.logical_and(jnp.min(low) > SAFE_LOW, jnp.max(high) < SAFE_HIGH).astype(jnp.int32)


def local_kernel(first, scalars, *refs):
    *pieces, keys, vals, state_ref, peak_ref, safe_ref, scores, weights = refs
    heads = state_ref.shape[0]
    full_tiles = scalars[0]
    row = token_rows(scalars[2], (BLOCK_QUERIES, TILE))
    col = lax.broadcasted_iota(jnp.int32, (BLOCK_QUERIES, TILE), 1)
    slant = col - row

    def tile_of(tile):
        return slice(tile * TILE, (tile + 1) * TILE)

    def unshifted(tiles, masked):
        span = tiles * TILE

        def weigh(g):
            q = stacked(pieces, first + g)
            for tile in range(tiles):
                s = scaled_scores(q, keys[:, tile_of(tile)])
                if tile >= masked:
                    s = jnp.where(slant <= (full_tiles - tile) * TILE, s, masked_score)
                weights[g % 2, :, tile_of(tile)] = jnp.exp2(s).astype(jnp.bfloat16)

        low = high = None
        weigh(0)
        for g in range(heads):
            if g + 1 < heads:
                weigh(g + 1)
            mixed = jnp.dot(weights[g % 2, :, 0:span], vals[0:span, :], preferred_element_type=jnp.float32)
            state_ref[g] = mixed
            peak_ref[g] = jnp.zeros(peak_ref.shape[1:], jnp.float32)
            total = mixed[:, HEAD_SIZE:]
            low = total if low is None else jnp.minimum(low, total)
            high = total if high is None else jnp.maximum(high, total)
        safe_ref[0] = is_safe(low, high)

    @pl.when(full_tiles == LOCAL_TILES - 1)
    def _():
        unshifted(LOCAL_TILES, LOCAL_TILES - 1)

    @pl.when(full_tiles < LOCAL_TILES - 1)
    def _():
        unshifted(LOCAL_TILES - 1, 0)

    @pl.when(safe_ref[0] == 0)
    def _():
        def tile_at(tile):
            return pl.ds(pl.multiple_of(tile * TILE, TILE), TILE)

        for g in range(heads):
            q = stacked(pieces, first + g)

            def score_tile(tile, peak):
                s = scaled_scores(q, keys[:, tile_at(tile)])
                s = jnp.where(slant <= (full_tiles - tile) * TILE, s, masked_score)
                scores[:, tile_at(tile)] = s
                return jnp.maximum(peak, jnp.max(s, axis=1, keepdims=True))

            peak = lax.fori_loop(0, full_tiles + 1, score_tile,
                                 jnp.full((BLOCK_QUERIES, 1), masked_score, jnp.float32))

            def mix_tile(tile, mixed):
                p = jnp.exp2(scores[:, tile_at(tile)] - peak).astype(jnp.bfloat16)
                return mixed + jnp.dot(p, vals[tile_at(tile), :], preferred_element_type=jnp.float32)

            state_ref[g] = lax.fori_loop(0, full_tiles + 1, mix_tile,
                                         jnp.zeros((BLOCK_QUERIES, 2 * HEAD_SIZE), jnp.float32))
            peak_ref[g] = jnp.broadcast_to(peak, peak_ref.shape[1:])


def anchor_kernel(scalars, early_safe, late_safe, moved, held, *refs):
    pieces, refs = refs[:KEY_HEADS], refs[KEY_HEADS:]
    states, refs = refs[:4], refs[4:]
    out_pieces, refs = refs[:KEY_HEADS], refs[KEY_HEADS:]
    anchor, keys, vals, weights, safe_ref = refs
    has_anchor = scalars[1] > 0
    choose_kernel(1, scalars, moved, held, anchor)
    widen_into(anchor, keys, vals)
    heads = []
    for state_ref, peak_ref in zip(states[0::2], states[1::2]):
        heads += [(state_ref.at[g], peak_ref.at[g]) for g in range(state_ref.shape[0])]

    def score(g):
        s = scaled_scores(stacked(pieces, g), keys[...])
        return jnp.where(has_anchor, s, masked_score)

    def mix(g):
        return jnp.dot(weights[g], vals[...], preferred_element_type=jnp.float32)

    def write(g, top, bottom):
        ratio = (top / bottom).astype(jnp.bfloat16)
        for k, piece in enumerate(out_pieces):
            piece[:, head_columns(g)] = ratio[k * ROWS:(k + 1) * ROWS]

    for g in range(GROUP):
        weights[g] = jnp.exp2(score(g)).astype(jnp.bfloat16)
    high = None
    for g, (state, _) in enumerate(heads):
        mixed = mix(g) + state[...]
        total = mixed[:, HEAD_SIZE:]
        write(g, mixed[:, :HEAD_SIZE], total)
        high = total if high is None else jnp.maximum(high, total)
    safe_ref[0] = is_safe(jnp.ones_like(high), high) * early_safe[0] * late_safe[0]

    @pl.when(safe_ref[0] == 0)
    def _():
        for g, (state, old) in enumerate(heads):
            s = score(g)
            peak = jnp.maximum(jnp.max(s, axis=1, keepdims=True), old[...])
            for at in range(0, ANCHOR_SLOTS, HEAD_SIZE):
                p = jnp.exp2(s[:, at:at + HEAD_SIZE] - peak)
                weights[g, :, at:at + HEAD_SIZE] = p.astype(jnp.bfloat16)
            mixed = mix(g)
            factor = jnp.exp2(old[...] - peak)
            write(g, mixed[:, :HEAD_SIZE] + state[:, :HEAD_SIZE] * factor,
                  mixed[:, HEAD_SIZE:] + state[:, HEAD_SIZE:] * factor)


def cost(heads, keys):
    flops = 4 * BLOCK_QUERIES * heads * keys * HEAD_SIZE
    return pl.CostEstimate(flops=flops, bytes_accessed=2 * 2**20, transcendentals=flops // 512)


smem = pl.BlockSpec(memory_space=pltpu.SMEM)
vmem = pl.BlockSpec(memory_space=pltpu.VMEM)
small = pltpu.CompilerParams(vmem_limit_bytes=4 * 2**20)
params = pltpu.CompilerParams(vmem_limit_bytes=24 * 2**20)
slight = pl.CostEstimate(flops=1000, bytes_accessed=1000, transcendentals=0)
safe_flag = jax.ShapeDtypeStruct((1,), jnp.int32)


def wide_shapes(count):
    return (jax.ShapeDtypeStruct((HEAD_SIZE, count), jnp.bfloat16),
            jax.ShapeDtypeStruct((count, 2 * HEAD_SIZE), jnp.bfloat16))


def piece_shape(rows):
    return jax.ShapeDtypeStruct((rows, GROUP * HEAD_SIZE), jnp.bfloat16)


def cut(scalars, queries):
    return pl.pallas_call(
        cut_kernel,
        out_shape=(piece_shape(queries.shape[0]),) * KEY_HEADS,
        in_specs=[smem, vmem],
        out_specs=(vmem,) * KEY_HEADS,
        compiler_params=small,
        cost_estimate=slight,
        name="cut",
    )(scalars, queries)


def join(scalars, pieces):
    rows, width = pieces[0].shape
    return pl.pallas_call(
        join_kernel,
        out_shape=jax.ShapeDtypeStruct((rows, KEY_HEADS * width), jnp.bfloat16),
        in_specs=[smem] + [vmem] * KEY_HEADS,
        out_specs=vmem,
        compiler_params=small,
        cost_estimate=slight,
        name="join",
    )(scalars, *pieces)


def choose(shift, scalars, moved, held):
    return pl.pallas_call(
        functools.partial(choose_kernel, shift),
        out_shape=jax.ShapeDtypeStruct(held.shape, held.dtype),
        in_specs=[smem, vmem, vmem],
        out_specs=vmem,
        compiler_params=small,
        cost_estimate=slight,
        name="choose",
    )(scalars, moved, held)


def widen(kv):
    return pl.pallas_call(
        widen_into,
        out_shape=wide_shapes(CACHE_SLOTS),
        in_specs=[vmem],
        out_specs=(vmem, vmem),
        compiler_params=params,
        cost_estimate=slight,
        name="widen",
    )(kv)


def attend_local(first, heads, scalars, pieces, keys, vals):
    return pl.pallas_call(
        functools.partial(local_kernel, first),
        out_shape=(
            jax.ShapeDtypeStruct((heads, BLOCK_QUERIES, 2 * HEAD_SIZE), jnp.float32),
            jax.ShapeDtypeStruct((heads, BLOCK_QUERIES, HEAD_SIZE), jnp.float32),
            safe_flag,
        ),
        in_specs=[smem] + [vmem] * (KEY_HEADS + 2),
        out_specs=(vmem, vmem, smem),
        scratch_shapes=[
            pltpu.VMEM((BLOCK_QUERIES, CACHE_SLOTS), jnp.float32),
            pltpu.VMEM((2, BLOCK_QUERIES, CACHE_SLOTS), jnp.bfloat16),
        ],
        compiler_params=params,
        cost_estimate=cost(GROUP, CACHE_SLOTS),
        name="attend_local",
    )(scalars, *pieces, keys, vals)


def attend_anchor(scalars, moved, held, pieces, early, late):
    states = (*early[:2], *late[:2])
    return pl.pallas_call(
        anchor_kernel,
        out_shape=(piece_shape(ROWS),) * KEY_HEADS,
        in_specs=[smem] * 3 + [vmem] * (2 + KEY_HEADS + len(states)),
        out_specs=(vmem,) * KEY_HEADS,
        scratch_shapes=[
            pltpu.VMEM(held.shape, held.dtype),
            *(pltpu.VMEM(wide.shape, wide.dtype) for wide in wide_shapes(ANCHOR_SLOTS)),
            pltpu.VMEM((GROUP, BLOCK_QUERIES, ANCHOR_SLOTS), jnp.bfloat16),
            pltpu.SMEM((1,), jnp.int32),
        ],
        compiler_params=params,
        cost_estimate=cost(GROUP, ANCHOR_SLOTS),
        name="attend_anchor",
    )(scalars, early[2], late[2], moved, held, *pieces, *states)


def body(queries, kv_cache, anchor_src, stretch_pos):
    block = lax.axis_index("ctx").astype(jnp.int32)
    mine = lax.axis_index("head").astype(jnp.int32)
    blocks = lax.axis_size("ctx")
    scalars = jnp.stack([stretch_pos[0] // TILE, block - anchor_src[0], mine])
    held, scalars, queries = lax.optimization_barrier((kv_cache[:, :ANCHOR_SLOTS, :], scalars, queries))

    def from_earlier(held, shift):
        return lax.ppermute(held, "ctx", [(b, b + shift) for b in range(blocks - shift)])

    def exchange(pieces):
        return [pieces[0]] + [
            lax.ppermute(pieces[k], "head", [(h, h ^ k) for h in range(KEY_HEADS)]) for k in range(1, KEY_HEADS)
        ]

    moved = from_earlier(held, 4)
    pieces = exchange(cut(scalars, queries))
    held = choose(4, scalars, moved, held)
    held, kv = lax.optimization_barrier((held, kv_cache))
    moved = from_earlier(held, 2)
    keys, vals = widen(kv)
    early = attend_local(0, FIRST_HEADS, scalars, pieces, keys, vals)
    moved, pieces, *early = lax.optimization_barrier((moved, pieces, *early))
    held = choose(2, scalars, moved, held)
    moved = from_earlier(held, 1)
    late = attend_local(FIRST_HEADS, GROUP - FIRST_HEADS, scalars, pieces, keys, vals)
    results = exchange(attend_anchor(scalars, moved, held, pieces, early, late))
    return join(scalars, results)


def solution(mesh):
    in_specs = (P(("ctx", "head"), None), P(None, "ctx", "head"), P("ctx"), P("ctx"))
    out_specs = P(("ctx", "head"), None)
    return jax.shard_map(body, mesh=mesh, in_specs=in_specs, out_specs=out_specs, check_vma=False)
```

```python
import functools
import math

import jax
import jax.numpy as jnp
from jax import lax
from jax.experimental import pallas as pl
from jax.experimental.pallas import tpu as pltpu
from jax.sharding import PartitionSpec as P

QUERY_HEAD_COUNT = 64
KEY_HEADS = 8
HEAD_SIZE = 128
GROUP = QUERY_HEAD_COUNT // KEY_HEADS
BLOCK_QUERIES = 256
CACHE_SLOTS = 2048
ANCHOR_SLOTS = 512
SPAN = 8
TILE = 256
STACK = 2
LOCAL_TILES = CACHE_SLOTS // TILE
ANCHOR_TILES = ANCHOR_SLOTS // TILE

masked_score = -1e30
EXP2_SCALE = math.log2(math.e) / math.sqrt(HEAD_SIZE)
SAFE_LOW, SAFE_HIGH = 2.0**-60, 2.0**60


def head_columns(g):
    return slice(g * HEAD_SIZE, (g + 1) * HEAD_SIZE)


def cut_kernel(queries, outgoing):
    pieces, _, width = outgoing.shape
    for h in range(pieces):
        outgoing[h] = queries[:, h * width:(h + 1) * width]


def choose_kernel(shift, scalars, moved, held, after, out):
    arrived = (scalars[1] & shift) != 0

    @pl.when(arrived)
    def _():
        out[...] = moved[...]

    @pl.when(jnp.logical_not(arrived))
    def _():
        out[...] = held[...]


def widen_kernel(part_ref, after, keys, vals):
    widen_into(part_ref, keys, vals)


def widen_into(part_ref, keys, vals):
    keys[...] = part_ref[0].astype(jnp.float32).T.astype(jnp.bfloat16)
    vals[:, 0:HEAD_SIZE] = part_ref[1]
    vals[:, HEAD_SIZE:] = jnp.ones(part_ref.shape[1:], jnp.bfloat16)


def scaled_scores(q, keys):
    return jnp.dot(q, keys, preferred_element_type=jnp.float32) * EXP2_SCALE


def is_safe(low, high):
    return jnp.logical_and(jnp.min(low) > SAFE_LOW, jnp.max(high) < SAFE_HIGH).astype(jnp.int32)


def stacked(q_ref, first):
    return jnp.concatenate([q_ref[:, head_columns(first + g)] for g in range(STACK)], axis=0)


def rows_of(g):
    return slice(g * BLOCK_QUERIES, (g + 1) * BLOCK_QUERIES)


def local_kernel(scalars, q_ref, keys, vals, state_ref, peak_ref, safe_ref, scores, weights):
    heads = state_ref.shape[0]
    full_tiles = scalars[0]
    row = lax.broadcasted_iota(jnp.int32, (BLOCK_QUERIES, TILE), 0)
    col = lax.broadcasted_iota(jnp.int32, (BLOCK_QUERIES, TILE), 1)
    slant = col - row

    def tile_of(tile):
        return slice(tile * TILE, (tile + 1) * TILE)

    def unshifted(tiles, masked):
        span = tiles * TILE

        def weigh(stack):
            q = stacked(q_ref, stack * STACK)
            for tile in range(tiles):
                s = scaled_scores(q, keys[:, tile_of(tile)])
                if tile >= masked:
                    allowed = slant <= (full_tiles - tile) * TILE
                    s = jnp.where(jnp.concatenate([allowed] * STACK, axis=0), s, masked_score)
                weights[stack % 2, :, tile_of(tile)] = jnp.exp2(s).astype(jnp.bfloat16)

        low = high = None
        weigh(0)
        for stack in range(heads // STACK):
            if (stack + 1) * STACK < heads:
                weigh(stack + 1)
            mixed = jnp.dot(weights[stack % 2, :, 0:span], vals[0:span, :], preferred_element_type=jnp.float32)
            for g in range(STACK):
                state_ref[stack * STACK + g] = mixed[rows_of(g)]
            total = mixed[:, HEAD_SIZE:]
            low = total if low is None else jnp.minimum(low, total)
            high = total if high is None else jnp.maximum(high, total)
        safe_ref[0] = is_safe(low, high)

    @pl.when(full_tiles == LOCAL_TILES - 1)
    def _():
        unshifted(LOCAL_TILES, LOCAL_TILES - 1)

    @pl.when(full_tiles < LOCAL_TILES - 1)
    def _():
        unshifted(LOCAL_TILES - 1, 0)

    @pl.when(safe_ref[0] == 0)
    def _():
        def tile_at(tile):
            return pl.ds(pl.multiple_of(tile * TILE, TILE), TILE)

        for g in range(heads):
            q = q_ref[:, head_columns(g)]

            def score_tile(tile, peak):
                s = scaled_scores(q, keys[:, tile_at(tile)])
                s = jnp.where(slant <= (full_tiles - tile) * TILE, s, masked_score)
                scores[:, tile_at(tile)] = s
                return jnp.maximum(peak, jnp.max(s, axis=1, keepdims=True))

            peak = lax.fori_loop(0, full_tiles + 1, score_tile,
                                 jnp.full((BLOCK_QUERIES, 1), masked_score, jnp.float32))

            def mix_tile(tile, mixed):
                p = jnp.exp2(scores[:, tile_at(tile)] - peak).astype(jnp.bfloat16)
                return mixed + jnp.dot(p, vals[tile_at(tile), :], preferred_element_type=jnp.float32)

            state_ref[g] = lax.fori_loop(0, full_tiles + 1, mix_tile,
                                         jnp.zeros((BLOCK_QUERIES, 2 * HEAD_SIZE), jnp.float32))
            peak_ref[g] = jnp.broadcast_to(peak, peak_ref.shape[1:])


def anchor_kernel(scalars, safe, moved, held, q_ref, states, peaks, out_ref, anchor, keys, vals, weights, safe_ref):
    heads = states.shape[0]
    has_anchor = scalars[1] > 0
    choose_kernel(1, scalars, moved, held, None, anchor)
    widen_into(anchor, keys, vals)

    def score(q):
        return jnp.where(has_anchor, scaled_scores(q, keys[...]), masked_score)

    def write(g, top, bottom):
        out_ref[:, head_columns(g)] = (top / bottom).astype(jnp.bfloat16)

    for stack in range(heads // STACK):
        weights[stack] = jnp.exp2(score(stacked(q_ref, stack * STACK))).astype(jnp.bfloat16)
    high = None
    for stack in range(heads // STACK):
        both = jnp.dot(weights[stack], vals[...], preferred_element_type=jnp.float32)
        for g in range(STACK):
            mixed = both[rows_of(g)] + states[stack * STACK + g]
            total = mixed[:, HEAD_SIZE:]
            write(stack * STACK + g, mixed[:, :HEAD_SIZE], total)
            high = total if high is None else jnp.maximum(high, total)
    safe_ref[0] = is_safe(jnp.ones_like(high), high) * safe[0]

    @pl.when(safe_ref[0] == 0)
    def _():
        for g in range(heads):
            s = score(q_ref[:, head_columns(g)])
            old = jnp.where(safe[0] == 1, 0.0, peaks[g])
            peak = jnp.maximum(jnp.max(s, axis=1, keepdims=True), old)
            for at in range(0, ANCHOR_SLOTS, HEAD_SIZE):
                p = jnp.exp2(s[:, at:at + HEAD_SIZE] - peak)
                weights[0, 0:BLOCK_QUERIES, at:at + HEAD_SIZE] = p.astype(jnp.bfloat16)
            mixed = jnp.dot(weights[0, 0:BLOCK_QUERIES], vals[...], preferred_element_type=jnp.float32)
            factor = jnp.exp2(old - peak)
            write(g, mixed[:, :HEAD_SIZE] + states[g, :, :HEAD_SIZE] * factor,
                  mixed[:, HEAD_SIZE:] + states[g, :, HEAD_SIZE:] * factor)


def cost(heads, keys):
    flops = 4 * BLOCK_QUERIES * heads * keys * HEAD_SIZE
    return pl.CostEstimate(flops=flops, bytes_accessed=2 * 2**20, transcendentals=flops // 512)


smem = pl.BlockSpec(memory_space=pltpu.SMEM)
vmem = pl.BlockSpec(memory_space=pltpu.VMEM)
anywhere = pl.BlockSpec(memory_space=pl.ANY)
small = pltpu.CompilerParams(vmem_limit_bytes=4 * 2**20)
params = pltpu.CompilerParams(vmem_limit_bytes=24 * 2**20)
slight = pl.CostEstimate(flops=1000, bytes_accessed=1000, transcendentals=0)
safe_flag = jax.ShapeDtypeStruct((1,), jnp.int32)


def wide_shapes(count):
    return (jax.ShapeDtypeStruct((HEAD_SIZE, count), jnp.bfloat16),
            jax.ShapeDtypeStruct((count, 2 * HEAD_SIZE), jnp.bfloat16))


def cut(queries):
    rows, width = queries.shape
    return pl.pallas_call(
        cut_kernel,
        out_shape=jax.ShapeDtypeStruct((KEY_HEADS, rows, width // KEY_HEADS), jnp.bfloat16),
        in_specs=[vmem],
        out_specs=vmem,
        compiler_params=small,
        cost_estimate=slight,
        name="cut",
    )(queries)


def choose(shift, scalars, moved, held, after):
    return pl.pallas_call(
        functools.partial(choose_kernel, shift),
        out_shape=jax.ShapeDtypeStruct(held.shape, held.dtype),
        in_specs=[smem, vmem, vmem, anywhere],
        out_specs=vmem,
        compiler_params=small,
        cost_estimate=slight,
        name="choose",
    )(scalars, moved, held, after)


def widen(kv, after):
    return pl.pallas_call(
        widen_kernel,
        out_shape=wide_shapes(CACHE_SLOTS),
        in_specs=[vmem, anywhere],
        out_specs=(vmem, vmem),
        compiler_params=params,
        cost_estimate=cost(GROUP, CACHE_SLOTS),
        name="widen",
    )(kv, after)


def attend_local(scalars, q, keys, vals):
    return pl.pallas_call(
        local_kernel,
        out_shape=(
            jax.ShapeDtypeStruct((GROUP, BLOCK_QUERIES, 2 * HEAD_SIZE), jnp.float32),
            jax.ShapeDtypeStruct((GROUP, BLOCK_QUERIES, HEAD_SIZE), jnp.float32),
            safe_flag,
        ),
        in_specs=[smem, vmem, vmem, vmem],
        out_specs=(vmem, vmem, smem),
        scratch_shapes=[
            pltpu.VMEM((BLOCK_QUERIES, CACHE_SLOTS), jnp.float32),
            pltpu.VMEM((2, STACK * BLOCK_QUERIES, CACHE_SLOTS), jnp.bfloat16),
        ],
        compiler_params=params,
        cost_estimate=cost(GROUP, CACHE_SLOTS),
        name="attend_local",
    )(scalars, q, keys, vals)


def attend_anchor(scalars, moved, held, q, states, peaks, safe):
    return pl.pallas_call(
        anchor_kernel,
        out_shape=jax.ShapeDtypeStruct(q.shape, jnp.bfloat16),
        in_specs=[smem] * 2 + [vmem] * 5,
        out_specs=vmem,
        scratch_shapes=[
            pltpu.VMEM(held.shape, held.dtype),
            *(pltpu.VMEM(wide.shape, wide.dtype) for wide in wide_shapes(ANCHOR_SLOTS)),
            pltpu.VMEM((GROUP // STACK, STACK * BLOCK_QUERIES, ANCHOR_SLOTS), jnp.bfloat16),
            pltpu.SMEM((1,), jnp.int32),
        ],
        compiler_params=params,
        cost_estimate=cost(GROUP, ANCHOR_SLOTS),
        name="attend_anchor",
    )(scalars, safe, moved, held, q, states, peaks)


def body(queries, kv_cache, anchor_src, stretch_pos):
    block = lax.axis_index("ctx").astype(jnp.int32)
    blocks = lax.axis_size("ctx")
    scalars = jnp.stack([stretch_pos[0] // TILE, block - anchor_src[0]])
    held, outgoing = lax.optimization_barrier((kv_cache[:, :ANCHOR_SLOTS, :], cut(queries)))

    def from_earlier(held, shift):
        return lax.ppermute(held, "ctx", [(b, b + shift) for b in range(blocks - shift)])

    moved = from_earlier(held, 4)
    q = lax.all_to_all(outgoing, "head", split_axis=0, concat_axis=0, tiled=True)
    q = q.reshape(BLOCK_QUERIES, GROUP * HEAD_SIZE)
    held = choose(4, scalars, moved, held, scalars)
    moved = from_earlier(held, 2)
    keys, vals = widen(kv_cache, q)
    held = choose(2, scalars, moved, held, keys)
    moved = from_earlier(held, 1)
    state = attend_local(scalars, q, keys, vals)
    result = attend_anchor(scalars, moved, held, q, *state)
    return lax.all_to_all(result, "head", split_axis=0, concat_axis=1, tiled=True)


def solution(mesh):
    in_specs = (P(("ctx", "head"), None), P(None, "ctx", "head"), P("ctx"), P("ctx"))
    out_specs = P(("ctx", "head"), None)
    return jax.shard_map(body, mesh=mesh, in_specs=in_specs, out_specs=out_specs, check_vma=False)
```

```python
import functools
import math

import jax
import jax.numpy as jnp
from jax import lax
from jax.experimental import pallas as pl
from jax.experimental.pallas import tpu as pltpu
from jax.sharding import PartitionSpec as P

QUERY_HEAD_COUNT = 64
KEY_HEADS = 8
HEAD_SIZE = 128
GROUP = QUERY_HEAD_COUNT // KEY_HEADS
BLOCK_QUERIES = 256
CACHE_SLOTS = 2048
ANCHOR_SLOTS = 512
SPAN = 8
TILE = 256
CHUNK = 512

masked_score = -1e30
EXP2_SCALE = math.log2(math.e) / math.sqrt(HEAD_SIZE)
SAFE_LOW, SAFE_HIGH = 2.0**-60, 2.0**60


def head_columns(g):
    return slice(g * HEAD_SIZE, (g + 1) * HEAD_SIZE)


def cut_kernel(queries, after, outgoing):
    pieces, _, width = outgoing.shape
    for h in range(pieces):
        outgoing[h] = queries[:, h * width:(h + 1) * width]


def choose_kernel(shift, scalars, moved, held, after, out):
    arrived = (scalars[1] & shift) != 0

    @pl.when(arrived)
    def _():
        out[...] = moved[...]

    @pl.when(jnp.logical_not(arrived))
    def _():
        out[...] = held[...]


def widen_kernel(part_ref, after, keys, vals):
    widen_into(part_ref, keys, vals)


def widen_into(part_ref, keys, vals):
    keys[...] = part_ref[0].astype(jnp.float32).T.astype(jnp.bfloat16)
    vals[:, 0:HEAD_SIZE] = part_ref[1]
    vals[:, HEAD_SIZE:] = jnp.ones(part_ref.shape[1:], jnp.bfloat16)


def scaled_scores(q, keys):
    return jnp.dot(q, keys, preferred_element_type=jnp.float32) * EXP2_SCALE


def is_safe(low, high):
    return jnp.logical_and(jnp.min(low) > SAFE_LOW, jnp.max(high) < SAFE_HIGH).astype(jnp.int32)


def sum_in_parts(weights, vals, span, parts=2):
    step = span // parts
    products = [
        jnp.dot(weights[:, i:i + step], vals[i:i + step, :], preferred_element_type=jnp.float32)
        for i in range(0, span, step)
    ]
    return functools.reduce(jnp.add, products)


def local_kernel(scalars, q_ref, keys, vals, state_ref, peak_ref, safe_ref, scores, weights):
    heads = state_ref.shape[0]
    full_tiles = scalars[0]
    row = lax.broadcasted_iota(jnp.int32, (BLOCK_QUERIES, CHUNK), 0)
    col = lax.broadcasted_iota(jnp.int32, (BLOCK_QUERIES, CHUNK), 1)
    slant = col - row

    def weigh(g, chunks):
        q = q_ref[:, head_columns(g)]
        for chunk in range(chunks):
            at = slice(chunk * CHUNK, (chunk + 1) * CHUNK)
            s = scaled_scores(q, keys[:, at])
            if chunk == chunks - 1:
                s = jnp.where(slant <= full_tiles * TILE - chunk * CHUNK, s, masked_score)
            weights[g % 2, :, at] = jnp.exp2(s).astype(jnp.bfloat16)

    def unshifted(chunks):
        weigh(0, chunks)
        for g in range(heads):
            if g + 1 < heads:
                weigh(g + 1, chunks)
            state_ref[g] = sum_in_parts(weights.at[g % 2], vals, chunks * CHUNK)

    for chunks in range(1, CACHE_SLOTS // CHUNK + 1):
        pl.when(full_tiles * TILE // CHUNK == chunks - 1)(functools.partial(unshifted, chunks))
    totals = [state_ref[g, :, HEAD_SIZE:] for g in range(heads)]
    safe_ref[0] = is_safe(functools.reduce(jnp.minimum, totals), functools.reduce(jnp.maximum, totals))

    @pl.when(safe_ref[0] == 0)
    def _():
        def tile_at(tile):
            return pl.ds(pl.multiple_of(tile * TILE, TILE), TILE)

        for g in range(heads):
            q = q_ref[:, head_columns(g)]

            def score_tile(tile, peak):
                s = scaled_scores(q, keys[:, tile_at(tile)])
                s = jnp.where(slant[:, :TILE] <= (full_tiles - tile) * TILE, s, masked_score)
                scores[:, tile_at(tile)] = s
                return jnp.maximum(peak, jnp.max(s, axis=1, keepdims=True))

            peak = lax.fori_loop(0, full_tiles + 1, score_tile,
                                 jnp.full((BLOCK_QUERIES, 1), masked_score, jnp.float32))

            def mix_tile(tile, mixed):
                p = jnp.exp2(scores[:, tile_at(tile)] - peak).astype(jnp.bfloat16)
                return mixed + jnp.dot(p, vals[tile_at(tile), :], preferred_element_type=jnp.float32)

            state_ref[g] = lax.fori_loop(0, full_tiles + 1, mix_tile,
                                         jnp.zeros((BLOCK_QUERIES, 2 * HEAD_SIZE), jnp.float32))
            peak_ref[g] = jnp.broadcast_to(peak, peak_ref.shape[1:])


def anchor_kernel(scalars, safe, moved, held, q_ref, states, peaks, out_ref, anchor, keys, vals, weights, safe_ref):
    heads = states.shape[0]
    has_anchor = scalars[1] > 0
    choose_kernel(1, scalars, moved, held, None, anchor)
    widen_into(anchor, keys, vals)

    def score(q):
        return jnp.where(has_anchor, scaled_scores(q, keys[...]), masked_score)

    def write(g, top, bottom):
        out_ref[:, head_columns(g)] = (top / bottom).astype(jnp.bfloat16)

    for g in range(heads):
        weights[g] = jnp.exp2(score(q_ref[:, head_columns(g)])).astype(jnp.bfloat16)
    high = None
    for g in range(heads):
        mixed = sum_in_parts(weights.at[g], vals, ANCHOR_SLOTS) + states[g]
        total = mixed[:, HEAD_SIZE:]
        write(g, mixed[:, :HEAD_SIZE], total)
        high = total if high is None else jnp.maximum(high, total)
    safe_ref[0] = is_safe(jnp.ones_like(high), high) * safe[0]

    @pl.when(safe_ref[0] == 0)
    def _():
        for g in range(heads):
            s = score(q_ref[:, head_columns(g)])
            old = jnp.where(safe[0] == 1, 0.0, peaks[g])
            peak = jnp.maximum(jnp.max(s, axis=1, keepdims=True), old)
            for at in range(0, ANCHOR_SLOTS, HEAD_SIZE):
                p = jnp.exp2(s[:, at:at + HEAD_SIZE] - peak)
                weights[g, :, at:at + HEAD_SIZE] = p.astype(jnp.bfloat16)
            mixed = jnp.dot(weights[g], vals[...], preferred_element_type=jnp.float32)
            factor = jnp.exp2(old - peak)
            write(g, mixed[:, :HEAD_SIZE] + states[g, :, :HEAD_SIZE] * factor,
                  mixed[:, HEAD_SIZE:] + states[g, :, HEAD_SIZE:] * factor)


def cost(heads, keys):
    flops = 4 * BLOCK_QUERIES * heads * keys * HEAD_SIZE
    return pl.CostEstimate(flops=flops, bytes_accessed=2 * 2**20, transcendentals=flops // 512)


smem = pl.BlockSpec(memory_space=pltpu.SMEM)
vmem = pl.BlockSpec(memory_space=pltpu.VMEM)
anywhere = pl.BlockSpec(memory_space=pl.ANY)
small = pltpu.CompilerParams(vmem_limit_bytes=4 * 2**20)
params = pltpu.CompilerParams(vmem_limit_bytes=24 * 2**20)
slight = pl.CostEstimate(flops=1000, bytes_accessed=1000, transcendentals=0)
safe_flag = jax.ShapeDtypeStruct((1,), jnp.int32)


def wide_shapes(count):
    return (jax.ShapeDtypeStruct((HEAD_SIZE, count), jnp.bfloat16),
            jax.ShapeDtypeStruct((count, 2 * HEAD_SIZE), jnp.bfloat16))


def cut(queries, after):
    rows, width = queries.shape
    return pl.pallas_call(
        cut_kernel,
        out_shape=jax.ShapeDtypeStruct((KEY_HEADS, rows, width // KEY_HEADS), jnp.bfloat16),
        in_specs=[vmem, anywhere],
        out_specs=vmem,
        compiler_params=small,
        cost_estimate=slight,
        name="cut",
    )(queries, after)


def choose(shift, scalars, moved, held, after, estimate):
    return pl.pallas_call(
        functools.partial(choose_kernel, shift),
        out_shape=jax.ShapeDtypeStruct(held.shape, held.dtype),
        in_specs=[smem, vmem, vmem, anywhere],
        out_specs=vmem,
        compiler_params=small,
        cost_estimate=estimate,
        name="choose",
    )(scalars, moved, held, after)


def widen(kv, after):
    return pl.pallas_call(
        widen_kernel,
        out_shape=wide_shapes(CACHE_SLOTS),
        in_specs=[vmem, anywhere],
        out_specs=(vmem, vmem),
        compiler_params=params,
        cost_estimate=cost(GROUP, CACHE_SLOTS),
        name="widen",
    )(kv, after)


def attend_local(scalars, q, keys, vals):
    return pl.pallas_call(
        local_kernel,
        out_shape=(
            jax.ShapeDtypeStruct((GROUP, BLOCK_QUERIES, 2 * HEAD_SIZE), jnp.float32),
            jax.ShapeDtypeStruct((GROUP, BLOCK_QUERIES, HEAD_SIZE), jnp.float32),
            safe_flag,
        ),
        in_specs=[smem, vmem, vmem, vmem],
        out_specs=(vmem, vmem, smem),
        scratch_shapes=[
            pltpu.VMEM((BLOCK_QUERIES, CACHE_SLOTS), jnp.float32),
            pltpu.VMEM((2, BLOCK_QUERIES, CACHE_SLOTS), jnp.bfloat16),
        ],
        compiler_params=params,
        cost_estimate=cost(GROUP, CACHE_SLOTS),
        name="attend_local",
    )(scalars, q, keys, vals)


def attend_anchor(scalars, moved, held, q, states, peaks, safe):
    return pl.pallas_call(
        anchor_kernel,
        out_shape=jax.ShapeDtypeStruct(q.shape, jnp.bfloat16),
        in_specs=[smem] * 2 + [vmem] * 5,
        out_specs=vmem,
        scratch_shapes=[
            pltpu.VMEM(held.shape, held.dtype),
            *(pltpu.VMEM(wide.shape, wide.dtype) for wide in wide_shapes(ANCHOR_SLOTS)),
            pltpu.VMEM((GROUP, BLOCK_QUERIES, ANCHOR_SLOTS), jnp.bfloat16),
            pltpu.SMEM((1,), jnp.int32),
        ],
        compiler_params=params,
        cost_estimate=cost(GROUP, ANCHOR_SLOTS),
        name="attend_anchor",
    )(scalars, safe, moved, held, q, states, peaks)


def body(queries, kv_cache, anchor_src, stretch_pos):
    block = lax.axis_index("ctx").astype(jnp.int32)
    blocks = lax.axis_size("ctx")
    scalars = jnp.stack([stretch_pos[0] // TILE, block - anchor_src[0]])
    held = lax.optimization_barrier(kv_cache[:, :ANCHOR_SLOTS, :])

    def from_earlier(held, shift):
        return lax.ppermute(held, "ctx", [(b, b + shift) for b in range(blocks - shift)])

    moved = from_earlier(held, 4)
    q = lax.all_to_all(cut(queries, held), "head", split_axis=0, concat_axis=0, tiled=True)
    q = q.reshape(BLOCK_QUERIES, GROUP * HEAD_SIZE)
    held = choose(4, scalars, moved, held, scalars, cost(GROUP, CACHE_SLOTS))
    moved = from_earlier(held, 2)
    keys, vals = widen(kv_cache, q)
    held = choose(2, scalars, moved, held, keys, slight)
    moved = from_earlier(held, 1)
    state = attend_local(scalars, q, keys, vals)
    result = attend_anchor(scalars, moved, held, q, *state)
    return lax.all_to_all(result, "head", split_axis=0, concat_axis=1, tiled=True)


def solution(mesh):
    in_specs = (P(("ctx", "head"), None), P(None, "ctx", "head"), P("ctx"), P("ctx"))
    out_specs = P(("ctx", "head"), None)
    return jax.shard_map(body, mesh=mesh, in_specs=in_specs, out_specs=out_specs, check_vma=False)
```

```python
import functools
import math

import jax
import jax.numpy as jnp
from jax import lax
from jax.experimental import pallas as pl
from jax.experimental.pallas import tpu as pltpu
from jax.sharding import PartitionSpec as P

QUERY_HEAD_COUNT = 64
KEY_HEADS = 8
HEAD_SIZE = 128
GROUP = QUERY_HEAD_COUNT // KEY_HEADS
BLOCK_QUERIES = 256
CACHE_SLOTS = 2048
ANCHOR_SLOTS = 512
SPAN = 8
TILE = 256
STACK = 2
CHUNK = 512

masked_score = -1e30
EXP2_SCALE = math.log2(math.e) / math.sqrt(HEAD_SIZE)
SAFE_LOW, SAFE_HIGH = 2.0**-60, 2.0**60


def head_columns(g):
    return slice(g * HEAD_SIZE, (g + 1) * HEAD_SIZE)


def cut_kernel(queries, after, outgoing):
    pieces, _, width = outgoing.shape
    for h in range(pieces):
        outgoing[h] = queries[:, h * width:(h + 1) * width]


def choose_kernel(shift, scalars, moved, held, after, out):
    arrived = (scalars[1] & shift) != 0

    @pl.when(arrived)
    def _():
        out[...] = moved[...]

    @pl.when(jnp.logical_not(arrived))
    def _():
        out[...] = held[...]


def widen_kernel(part_ref, after, keys, vals):
    widen_into(part_ref, keys, vals)


def widen_into(part_ref, keys, vals):
    keys[...] = part_ref[0].astype(jnp.float32).T.astype(jnp.bfloat16)
    vals[:, 0:HEAD_SIZE] = part_ref[1]
    vals[:, HEAD_SIZE:] = jnp.ones(part_ref.shape[1:], jnp.bfloat16)


def scaled_scores(q, keys):
    return jnp.dot(q, keys, preferred_element_type=jnp.float32) * EXP2_SCALE


def stacked(q_ref, stack):
    return jnp.concatenate([q_ref[:, head_columns(stack * STACK + g)] for g in range(STACK)], axis=0)


def rows_of(g):
    return slice(g * BLOCK_QUERIES, (g + 1) * BLOCK_QUERIES)


def tile_of(tile):
    return slice(tile * TILE, (tile + 1) * TILE)


def tile_at(tile):
    return pl.ds(pl.multiple_of(tile * TILE, TILE), TILE)


def causal_slant():
    row = lax.broadcasted_iota(jnp.int32, (BLOCK_QUERIES, TILE), 0)
    col = lax.broadcasted_iota(jnp.int32, (BLOCK_QUERIES, TILE), 1)
    return col - row


def local_kernel(scalars, q_ref, keys, vals, state_ref, weights):
    stacks = state_ref.shape[0] // STACK
    full_tiles = scalars[0]
    slant = causal_slant()

    def attend(chunks):
        span = chunks * CHUNK
        tiles = span // TILE

        def weigh(stack):
            q = stacked(q_ref, stack)
            for tile in range(tiles):
                s = scaled_scores(q, keys[:, tile_of(tile)])
                if tile * TILE >= span - CHUNK:
                    allowed = slant <= (full_tiles - tile) * TILE
                    s = jnp.where(jnp.concatenate([allowed] * STACK, axis=0), s, masked_score)
                weights[stack % 2, :, tile_of(tile)] = jnp.exp2(s).astype(jnp.bfloat16)

        weigh(0)
        for stack in range(stacks):
            if stack + 1 < stacks:
                weigh(stack + 1)
            mixed = jnp.dot(weights[stack % 2, :, 0:span], vals[0:span, :], preferred_element_type=jnp.float32)
            for g in range(STACK):
                state_ref[stack * STACK + g] = mixed[rows_of(g)]

    for chunks in range(1, CACHE_SLOTS // CHUNK + 1):
        pl.when(full_tiles * TILE // CHUNK == chunks - 1)(functools.partial(attend, chunks))


def exact_head(g, full_tiles, has_anchor, q_ref, local, anchor, scores):
    q = q_ref[:, head_columns(g)]
    slant = causal_slant()
    base = ANCHOR_SLOTS // TILE
    zero = jnp.zeros((BLOCK_QUERIES, 2 * HEAD_SIZE), jnp.float32)

    def score_into(slot, keys, tile, allowed, peak):
        s = jnp.where(allowed, scaled_scores(q, keys[:, tile_at(tile)]), masked_score)
        scores[:, tile_at(slot + tile)] = s
        return jnp.maximum(peak, jnp.max(s, axis=1, keepdims=True))

    def mix_from(slot, vals, tile, mixed):
        p = jnp.exp2(scores[:, tile_at(slot + tile)] - peak).astype(jnp.bfloat16)
        return mixed + jnp.dot(p, vals[tile_at(tile), :], preferred_element_type=jnp.float32)

    peak = jnp.full((BLOCK_QUERIES, 1), masked_score, jnp.float32)
    peak = lax.fori_loop(
        0, full_tiles + 1,
        lambda tile, peak: score_into(base, local[0], tile, slant <= (full_tiles - tile) * TILE, peak), peak)
    peak = lax.fori_loop(
        0, base, lambda tile, peak: score_into(0, anchor[0], tile, jnp.logical_and(has_anchor, slant == slant), peak),
        peak)
    mixed = lax.fori_loop(0, full_tiles + 1, functools.partial(mix_from, base, local[1]), zero)
    return lax.fori_loop(0, base, functools.partial(mix_from, 0, anchor[1]), mixed)


def anchor_kernel(scalars, moved, held, q_ref, local_keys, local_vals, states, out_ref,
                  anchor, keys, vals, weights, scores):
    heads = states.shape[0]
    has_anchor = scalars[1] > 0
    choose_kernel(1, scalars, moved, held, None, anchor)
    widen_into(anchor, keys, vals)

    def write(g, mixed):
        out_ref[:, head_columns(g)] = (mixed[:, :HEAD_SIZE] / mixed[:, HEAD_SIZE:]).astype(jnp.bfloat16)

    for stack in range(heads // STACK):
        s = jnp.where(has_anchor, scaled_scores(stacked(q_ref, stack), keys[...]), masked_score)
        weights[stack] = jnp.exp2(s).astype(jnp.bfloat16)
    low = high = None
    for stack in range(heads // STACK):
        both = jnp.dot(weights[stack], vals[...], preferred_element_type=jnp.float32)
        for g in range(STACK):
            state = states[stack * STACK + g]
            mixed = both[rows_of(g)] + state
            write(stack * STACK + g, mixed)
            below, above = state[:, HEAD_SIZE:], mixed[:, HEAD_SIZE:]
            low = below if low is None else jnp.minimum(low, below)
            high = above if high is None else jnp.maximum(high, above)
    safe = jnp.logical_and(jnp.min(low) > SAFE_LOW, jnp.max(high) < SAFE_HIGH)

    @pl.when(jnp.logical_not(safe))
    def _():
        for g in range(heads):
            write(g, exact_head(g, scalars[0], has_anchor, q_ref, (local_keys, local_vals), (keys, vals), scores))


def cost(heads, keys):
    flops = 4 * BLOCK_QUERIES * heads * keys * HEAD_SIZE
    return pl.CostEstimate(flops=flops, bytes_accessed=2 * 2**20, transcendentals=flops // 512)


smem = pl.BlockSpec(memory_space=pltpu.SMEM)
vmem = pl.BlockSpec(memory_space=pltpu.VMEM)
anywhere = pl.BlockSpec(memory_space=pl.ANY)
small = pltpu.CompilerParams(vmem_limit_bytes=4 * 2**20)
params = pltpu.CompilerParams(vmem_limit_bytes=24 * 2**20)
slight = pl.CostEstimate(flops=1000, bytes_accessed=1000, transcendentals=0)


def wide_shapes(count):
    return (jax.ShapeDtypeStruct((HEAD_SIZE, count), jnp.bfloat16),
            jax.ShapeDtypeStruct((count, 2 * HEAD_SIZE), jnp.bfloat16))


def cut(queries, after):
    rows, width = queries.shape
    return pl.pallas_call(
        cut_kernel,
        out_shape=jax.ShapeDtypeStruct((KEY_HEADS, rows, width // KEY_HEADS), jnp.bfloat16),
        in_specs=[vmem, anywhere],
        out_specs=vmem,
        compiler_params=small,
        cost_estimate=slight,
        name="cut",
    )(queries, after)


def choose(shift, scalars, moved, held, after, estimate):
    return pl.pallas_call(
        functools.partial(choose_kernel, shift),
        out_shape=jax.ShapeDtypeStruct(held.shape, held.dtype),
        in_specs=[smem, vmem, vmem, anywhere],
        out_specs=vmem,
        compiler_params=small,
        cost_estimate=estimate,
        name="choose",
    )(scalars, moved, held, after)


def widen(kv, after):
    return pl.pallas_call(
        widen_kernel,
        out_shape=wide_shapes(CACHE_SLOTS),
        in_specs=[vmem, anywhere],
        out_specs=(vmem, vmem),
        compiler_params=params,
        cost_estimate=cost(GROUP, CACHE_SLOTS),
        name="widen",
    )(kv, after)


def attend_local(scalars, q, keys, vals):
    return pl.pallas_call(
        local_kernel,
        out_shape=jax.ShapeDtypeStruct((GROUP, BLOCK_QUERIES, 2 * HEAD_SIZE), jnp.float32),
        in_specs=[smem, vmem, vmem, vmem],
        out_specs=vmem,
        scratch_shapes=[pltpu.VMEM((2, STACK * BLOCK_QUERIES, CACHE_SLOTS), jnp.bfloat16)],
        compiler_params=params,
        cost_estimate=cost(GROUP, CACHE_SLOTS),
        name="attend_local",
    )(scalars, q, keys, vals)


def attend_anchor(scalars, moved, held, q, keys, vals, states):
    return pl.pallas_call(
        anchor_kernel,
        out_shape=jax.ShapeDtypeStruct(q.shape, jnp.bfloat16),
        in_specs=[smem] + [vmem] * 6,
        out_specs=vmem,
        scratch_shapes=[
            pltpu.VMEM(held.shape, held.dtype),
            *(pltpu.VMEM(wide.shape, wide.dtype) for wide in wide_shapes(ANCHOR_SLOTS)),
            pltpu.VMEM((GROUP // STACK, STACK * BLOCK_QUERIES, ANCHOR_SLOTS), jnp.bfloat16),
            pltpu.VMEM((BLOCK_QUERIES, ANCHOR_SLOTS + CACHE_SLOTS), jnp.float32),
        ],
        compiler_params=params,
        cost_estimate=cost(GROUP, ANCHOR_SLOTS),
        name="attend_anchor",
    )(scalars, moved, held, q, keys, vals, states)


def body(queries, kv_cache, anchor_src, stretch_pos):
    block = lax.axis_index("ctx").astype(jnp.int32)
    blocks = lax.axis_size("ctx")
    scalars = jnp.stack([stretch_pos[0] // TILE, block - anchor_src[0]])
    held = lax.optimization_barrier(kv_cache[:, :ANCHOR_SLOTS, :])

    def from_earlier(held, shift):
        return lax.ppermute(held, "ctx", [(b, b + shift) for b in range(blocks - shift)])

    moved = from_earlier(held, 4)
    q = lax.all_to_all(cut(queries, held), "head", split_axis=0, concat_axis=0, tiled=True)
    q = q.reshape(BLOCK_QUERIES, GROUP * HEAD_SIZE)
    held = choose(4, scalars, moved, held, scalars, cost(GROUP, CACHE_SLOTS))
    moved = from_earlier(held, 2)
    keys, vals = widen(kv_cache, q)
    held = choose(2, scalars, moved, held, keys, slight)
    moved = from_earlier(held, 1)
    states = attend_local(scalars, q, keys, vals)
    result = attend_anchor(scalars, moved, held, q, keys, vals, states)
    return lax.all_to_all(result, "head", split_axis=0, concat_axis=1, tiled=True)


def solution(mesh):
    in_specs = (P(("ctx", "head"), None), P(None, "ctx", "head"), P("ctx"), P("ctx"))
    out_specs = P(("ctx", "head"), None)
    return jax.shard_map(body, mesh=mesh, in_specs=in_specs, out_specs=out_specs, check_vma=False)
```

```python
import functools
import math

import jax
import jax.numpy as jnp
from jax import lax
from jax.experimental import pallas as pl
from jax.experimental.pallas import tpu as pltpu
from jax.sharding import PartitionSpec as P

QUERY_HEAD_COUNT = 64
KEY_HEADS = 8
HEAD_SIZE = 128
GROUP = QUERY_HEAD_COUNT // KEY_HEADS
BLOCK_QUERIES = 256
CACHE_SLOTS = 2048
ANCHOR_SLOTS = 512
SPAN = 8
TILE = 256
STACK = 2
CHUNK = 512

masked_score = -1e30
EXP2_SCALE = math.log2(math.e) / math.sqrt(HEAD_SIZE)
SAFE_LOW, SAFE_HIGH = 2.0**-60, 2.0**60


def head_columns(g):
    return slice(g * HEAD_SIZE, (g + 1) * HEAD_SIZE)


def cut_kernel(queries, after, outgoing):
    pieces, _, width = outgoing.shape
    for h in range(pieces):
        outgoing[h] = queries[:, h * width:(h + 1) * width]


def choose_kernel(shift, scalars, moved, held, after, out):
    arrived = (scalars[1] & shift) != 0

    @pl.when(arrived)
    def _():
        out[...] = moved[...]

    @pl.when(jnp.logical_not(arrived))
    def _():
        out[...] = held[...]


def widen_kernel(part_ref, after, keys, vals):
    widen_into(part_ref, keys, vals)


def widen_into(part_ref, keys, vals):
    keys[...] = part_ref[0].astype(jnp.float32).T.astype(jnp.bfloat16)
    vals[:, 0:HEAD_SIZE] = part_ref[1]
    vals[:, HEAD_SIZE:] = jnp.ones(part_ref.shape[1:], jnp.bfloat16)


def scaled_scores(q, keys):
    return jnp.dot(q, keys, preferred_element_type=jnp.float32) * EXP2_SCALE


def stacked(q_ref, stack):
    return jnp.concatenate([q_ref[:, head_columns(stack * STACK + g)] for g in range(STACK)], axis=0)


def rows_of(g):
    return slice(g * BLOCK_QUERIES, (g + 1) * BLOCK_QUERIES)


def tile_of(tile):
    return slice(tile * TILE, (tile + 1) * TILE)


def tile_at(tile):
    return pl.ds(pl.multiple_of(tile * TILE, TILE), TILE)


def causal_slant():
    row = lax.broadcasted_iota(jnp.int32, (BLOCK_QUERIES, TILE), 0)
    col = lax.broadcasted_iota(jnp.int32, (BLOCK_QUERIES, TILE), 1)
    return col - row


def local_kernel(scalars, q_ref, keys, vals, state_ref, weights):
    stacks = state_ref.shape[0] // STACK
    full_tiles = scalars[0]
    slant = causal_slant()

    def attend(chunks):
        span = chunks * CHUNK
        tiles = span // TILE

        def weigh(stack):
            q = stacked(q_ref, stack)
            for tile in range(tiles):
                s = scaled_scores(q, keys[:, tile_of(tile)])
                if tile * TILE >= span - CHUNK:
                    allowed = slant <= (full_tiles - tile) * TILE
                    s = jnp.where(jnp.concatenate([allowed] * STACK, axis=0), s, masked_score)
                weights[stack % 2, :, tile_of(tile)] = jnp.exp2(s).astype(jnp.bfloat16)

        weigh(0)
        for stack in range(stacks):
            if stack + 1 < stacks:
                weigh(stack + 1)
            mixed = jnp.dot(weights[stack % 2, :, 0:span], vals[0:span, :], preferred_element_type=jnp.float32)
            for g in range(STACK):
                state_ref[stack * STACK + g] = mixed[rows_of(g)]

    for chunks in range(1, CACHE_SLOTS // CHUNK + 1):
        pl.when(full_tiles * TILE // CHUNK == chunks - 1)(functools.partial(attend, chunks))


def exact_head(g, full_tiles, has_anchor, q_ref, local, anchor, scores):
    q = q_ref[:, head_columns(g)]
    slant = causal_slant()
    base = ANCHOR_SLOTS // TILE
    zero = jnp.zeros((BLOCK_QUERIES, 2 * HEAD_SIZE), jnp.float32)

    def score_into(slot, keys, tile, allowed, peak):
        s = jnp.where(allowed, scaled_scores(q, keys[:, tile_at(tile)]), masked_score)
        scores[:, tile_at(slot + tile)] = s
        return jnp.maximum(peak, jnp.max(s, axis=1, keepdims=True))

    def mix_from(slot, vals, tile, mixed):
        p = jnp.exp2(scores[:, tile_at(slot + tile)] - peak).astype(jnp.bfloat16)
        return mixed + jnp.dot(p, vals[tile_at(tile), :], preferred_element_type=jnp.float32)

    peak = jnp.full((BLOCK_QUERIES, 1), masked_score, jnp.float32)
    peak = lax.fori_loop(
        0, full_tiles + 1,
        lambda tile, peak: score_into(base, local[0], tile, slant <= (full_tiles - tile) * TILE, peak), peak)
    peak = lax.fori_loop(
        0, base, lambda tile, peak: score_into(0, anchor[0], tile, jnp.logical_and(has_anchor, slant == slant), peak),
        peak)
    mixed = lax.fori_loop(0, full_tiles + 1, functools.partial(mix_from, base, local[1]), zero)
    return lax.fori_loop(0, base, functools.partial(mix_from, 0, anchor[1]), mixed)


def anchor_kernel(scalars, moved, held, q_ref, local_keys, local_vals, states, out_ref,
                  anchor, keys, vals, weights, scores):
    heads = states.shape[0]
    has_anchor = scalars[1] > 0
    choose_kernel(1, scalars, moved, held, None, anchor)
    widen_into(anchor, keys, vals)

    def write(g, mixed):
        out_ref[:, head_columns(g)] = (mixed[:, :HEAD_SIZE] / mixed[:, HEAD_SIZE:]).astype(jnp.bfloat16)

    for stack in range(heads // STACK):
        s = jnp.where(has_anchor, scaled_scores(stacked(q_ref, stack), keys[...]), masked_score)
        weights[stack] = jnp.exp2(s).astype(jnp.bfloat16)
    low = high = None
    for stack in range(heads // STACK):
        both = jnp.dot(weights[stack], vals[...], preferred_element_type=jnp.float32)
        for g in range(STACK):
            state = states[stack * STACK + g]
            mixed = both[rows_of(g)] + state
            write(stack * STACK + g, mixed)
            below, above = state[:, HEAD_SIZE:], mixed[:, HEAD_SIZE:]
            low = below if low is None else jnp.minimum(low, below)
            high = above if high is None else jnp.maximum(high, above)
    safe = jnp.logical_and(jnp.min(low) > SAFE_LOW, jnp.max(high) < SAFE_HIGH)

    @pl.when(jnp.logical_not(safe))
    def _():
        for g in range(heads):
            write(g, exact_head(g, scalars[0], has_anchor, q_ref, (local_keys, local_vals), (keys, vals), scores))


def cost(heads, keys):
    flops = 4 * BLOCK_QUERIES * heads * keys * HEAD_SIZE
    return pl.CostEstimate(flops=flops, bytes_accessed=2 * 2**20, transcendentals=flops // 512)


smem = pl.BlockSpec(memory_space=pltpu.SMEM)
vmem = pl.BlockSpec(memory_space=pltpu.VMEM)
anywhere = pl.BlockSpec(memory_space=pl.ANY)
small = pltpu.CompilerParams(vmem_limit_bytes=4 * 2**20)
params = pltpu.CompilerParams(vmem_limit_bytes=24 * 2**20)
slight = pl.CostEstimate(flops=1000, bytes_accessed=1000, transcendentals=0)


def wide_shapes(count):
    return (jax.ShapeDtypeStruct((HEAD_SIZE, count), jnp.bfloat16),
            jax.ShapeDtypeStruct((count, 2 * HEAD_SIZE), jnp.bfloat16))


def cut(queries, after):
    rows, width = queries.shape
    return pl.pallas_call(
        cut_kernel,
        out_shape=jax.ShapeDtypeStruct((KEY_HEADS, rows, width // KEY_HEADS), jnp.bfloat16),
        in_specs=[vmem, anywhere],
        out_specs=vmem,
        compiler_params=small,
        cost_estimate=slight,
        name="cut",
    )(queries, after)


def choose(shift, scalars, moved, held, after, estimate):
    return pl.pallas_call(
        functools.partial(choose_kernel, shift),
        out_shape=jax.ShapeDtypeStruct(held.shape, held.dtype),
        in_specs=[smem, vmem, vmem, anywhere],
        out_specs=vmem,
        compiler_params=small,
        cost_estimate=estimate,
        name="choose",
    )(scalars, moved, held, after)


def widen(kv, after):
    return pl.pallas_call(
        widen_kernel,
        out_shape=wide_shapes(CACHE_SLOTS),
        in_specs=[vmem, anywhere],
        out_specs=(vmem, vmem),
        compiler_params=params,
        cost_estimate=cost(GROUP, CACHE_SLOTS),
        name="widen",
    )(kv, after)


def attend_local(scalars, q, keys, vals):
    return pl.pallas_call(
        local_kernel,
        out_shape=jax.ShapeDtypeStruct((GROUP, BLOCK_QUERIES, 2 * HEAD_SIZE), jnp.float32),
        in_specs=[smem, vmem, vmem, vmem],
        out_specs=vmem,
        scratch_shapes=[pltpu.VMEM((2, STACK * BLOCK_QUERIES, CACHE_SLOTS), jnp.bfloat16)],
        compiler_params=params,
        cost_estimate=cost(GROUP, CACHE_SLOTS),
        name="attend_local",
    )(scalars, q, keys, vals)


def attend_anchor(scalars, moved, held, q, keys, vals, states):
    return pl.pallas_call(
        anchor_kernel,
        out_shape=jax.ShapeDtypeStruct(q.shape, jnp.bfloat16),
        in_specs=[smem] + [vmem] * 6,
        out_specs=vmem,
        scratch_shapes=[
            pltpu.VMEM(held.shape, held.dtype),
            *(pltpu.VMEM(wide.shape, wide.dtype) for wide in wide_shapes(ANCHOR_SLOTS)),
            pltpu.VMEM((GROUP // STACK, STACK * BLOCK_QUERIES, ANCHOR_SLOTS), jnp.bfloat16),
            pltpu.VMEM((BLOCK_QUERIES, ANCHOR_SLOTS + CACHE_SLOTS), jnp.float32),
        ],
        compiler_params=params,
        cost_estimate=cost(GROUP, ANCHOR_SLOTS),
        name="attend_anchor",
    )(scalars, moved, held, q, keys, vals, states)


def body(queries, kv_cache, anchor_src, stretch_pos):
    block = lax.axis_index("ctx").astype(jnp.int32)
    blocks = lax.axis_size("ctx")
    scalars = jnp.stack([stretch_pos[0] // TILE, block - anchor_src[0]])
    held = lax.optimization_barrier(kv_cache[:, :ANCHOR_SLOTS, :])

    def from_earlier(held, shift):
        return lax.ppermute(held, "ctx", [(b, b + shift) for b in range(blocks - shift)])

    moved = from_earlier(held, 2)
    q = lax.all_to_all(cut(queries, held), "head", split_axis=0, concat_axis=0, tiled=True)
    q = q.reshape(BLOCK_QUERIES, GROUP * HEAD_SIZE)
    held = choose(2, scalars, moved, held, scalars, cost(GROUP, CACHE_SLOTS))
    moved = from_earlier(held, 4)
    keys, vals = widen(kv_cache, held)
    held = choose(4, scalars, moved, held, keys, slight)
    moved = from_earlier(held, 1)
    states = attend_local(scalars, q, keys, vals)
    result = attend_anchor(scalars, moved, held, q, keys, vals, states)
    return lax.all_to_all(result, "head", split_axis=0, concat_axis=1, tiled=True)


def solution(mesh):
    in_specs = (P(("ctx", "head"), None), P(None, "ctx", "head"), P("ctx"), P("ctx"))
    out_specs = P(("ctx", "head"), None)
    return jax.shard_map(body, mesh=mesh, in_specs=in_specs, out_specs=out_specs, check_vma=False)
```

```python
import functools
import math

import jax
import jax.numpy as jnp
from jax import lax
from jax.experimental import pallas as pl
from jax.experimental.pallas import tpu as pltpu
from jax.sharding import PartitionSpec as P

QUERY_HEAD_COUNT = 64
KEY_HEADS = 8
HEAD_SIZE = 128
GROUP = QUERY_HEAD_COUNT // KEY_HEADS
BLOCK_QUERIES = 256
CACHE_SLOTS = 2048
ANCHOR_SLOTS = 512
SPAN = 8
TILE = 256
STACK = 2
CHUNK = 512

masked_score = -1e30
EXP2_SCALE = math.log2(math.e) / math.sqrt(HEAD_SIZE)
SAFE_LOW, SAFE_HIGH = 2.0**-60, 2.0**60


def head_columns(g):
    return slice(g * HEAD_SIZE, (g + 1) * HEAD_SIZE)


def cut_kernel(queries, after, outgoing):
    pieces, _, width = outgoing.shape
    for h in range(pieces):
        outgoing[h] = queries[:, h * width:(h + 1) * width]


def full_tiles_of(facts):
    return jnp.max(facts[0])


def place_of(facts):
    return jnp.max(facts[1])


def choose_kernel(shift, facts, moved, held, after, out):
    arrived = (place_of(facts) & shift) != 0

    @pl.when(arrived)
    def _():
        out[...] = moved[...]

    @pl.when(jnp.logical_not(arrived))
    def _():
        out[...] = held[...]


def widen_kernel(part_ref, after, keys, vals):
    widen_into(part_ref, keys, vals)


def widen_into(part_ref, keys, vals):
    keys[...] = part_ref[0].astype(jnp.float32).T.astype(jnp.bfloat16)
    vals[:, 0:HEAD_SIZE] = part_ref[1]
    vals[:, HEAD_SIZE:] = jnp.ones(part_ref.shape[1:], jnp.bfloat16)


def scaled_scores(q, keys):
    return jnp.dot(q, keys, preferred_element_type=jnp.float32) * EXP2_SCALE


def stacked(q_ref, stack):
    return jnp.concatenate([q_ref[:, head_columns(stack * STACK + g)] for g in range(STACK)], axis=0)


def rows_of(g):
    return slice(g * BLOCK_QUERIES, (g + 1) * BLOCK_QUERIES)


def tile_of(tile):
    return slice(tile * TILE, (tile + 1) * TILE)


def tile_at(tile):
    return pl.ds(pl.multiple_of(tile * TILE, TILE), TILE)


def causal_slant():
    row = lax.broadcasted_iota(jnp.int32, (BLOCK_QUERIES, TILE), 0)
    col = lax.broadcasted_iota(jnp.int32, (BLOCK_QUERIES, TILE), 1)
    return col - row


def local_kernel(facts, q_ref, keys, vals, state_ref, weights):
    stacks = state_ref.shape[0] // STACK
    full_tiles = full_tiles_of(facts)
    slant = causal_slant()

    def attend(chunks):
        span = chunks * CHUNK
        tiles = span // TILE

        def weigh(stack):
            q = stacked(q_ref, stack)
            for tile in range(tiles):
                s = scaled_scores(q, keys[:, tile_of(tile)])
                if tile * TILE >= span - CHUNK:
                    allowed = slant <= (full_tiles - tile) * TILE
                    s = jnp.where(jnp.concatenate([allowed] * STACK, axis=0), s, masked_score)
                weights[stack % 2, :, tile_of(tile)] = jnp.exp2(s).astype(jnp.bfloat16)

        weigh(0)
        for stack in range(stacks):
            if stack + 1 < stacks:
                weigh(stack + 1)
            mixed = jnp.dot(weights[stack % 2, :, 0:span], vals[0:span, :], preferred_element_type=jnp.float32)
            for g in range(STACK):
                state_ref[stack * STACK + g] = mixed[rows_of(g)]

    for chunks in range(1, CACHE_SLOTS // CHUNK + 1):
        pl.when(full_tiles * TILE // CHUNK == chunks - 1)(functools.partial(attend, chunks))


def exact_head(g, full_tiles, has_anchor, q_ref, local, anchor, scores):
    q = q_ref[:, head_columns(g)]
    slant = causal_slant()
    base = ANCHOR_SLOTS // TILE
    zero = jnp.zeros((BLOCK_QUERIES, 2 * HEAD_SIZE), jnp.float32)

    def score_into(slot, keys, tile, allowed, peak):
        s = jnp.where(allowed, scaled_scores(q, keys[:, tile_at(tile)]), masked_score)
        scores[:, tile_at(slot + tile)] = s
        return jnp.maximum(peak, jnp.max(s, axis=1, keepdims=True))

    def mix_from(slot, vals, tile, mixed):
        p = jnp.exp2(scores[:, tile_at(slot + tile)] - peak).astype(jnp.bfloat16)
        return mixed + jnp.dot(p, vals[tile_at(tile), :], preferred_element_type=jnp.float32)

    peak = jnp.full((BLOCK_QUERIES, 1), masked_score, jnp.float32)
    peak = lax.fori_loop(
        0, full_tiles + 1,
        lambda tile, peak: score_into(base, local[0], tile, slant <= (full_tiles - tile) * TILE, peak), peak)
    peak = lax.fori_loop(
        0, base, lambda tile, peak: score_into(0, anchor[0], tile, jnp.logical_and(has_anchor, slant == slant), peak),
        peak)
    mixed = lax.fori_loop(0, full_tiles + 1, functools.partial(mix_from, base, local[1]), zero)
    return lax.fori_loop(0, base, functools.partial(mix_from, 0, anchor[1]), mixed)


def anchor_kernel(facts, moved, held, q_ref, local_keys, local_vals, states, out_ref,
                  anchor, keys, vals, weights, scores):
    heads = states.shape[0]
    has_anchor = place_of(facts) > 0
    choose_kernel(1, facts, moved, held, None, anchor)
    widen_into(anchor, keys, vals)

    def write(g, mixed):
        out_ref[:, head_columns(g)] = (mixed[:, :HEAD_SIZE] / mixed[:, HEAD_SIZE:]).astype(jnp.bfloat16)

    for stack in range(heads // STACK):
        s = jnp.where(has_anchor, scaled_scores(stacked(q_ref, stack), keys[...]), masked_score)
        weights[stack] = jnp.exp2(s).astype(jnp.bfloat16)
    low = high = None
    for stack in range(heads // STACK):
        both = jnp.dot(weights[stack], vals[...], preferred_element_type=jnp.float32)
        for g in range(STACK):
            state = states[stack * STACK + g]
            mixed = both[rows_of(g)] + state
            write(stack * STACK + g, mixed)
            below, above = state[:, HEAD_SIZE:], mixed[:, HEAD_SIZE:]
            low = below if low is None else jnp.minimum(low, below)
            high = above if high is None else jnp.maximum(high, above)
    safe = jnp.logical_and(jnp.min(low) > SAFE_LOW, jnp.max(high) < SAFE_HIGH)

    @pl.when(jnp.logical_not(safe))
    def _():
        for g in range(heads):
            write(g, exact_head(g, full_tiles_of(facts), has_anchor, q_ref, (local_keys, local_vals), (keys, vals), scores))


def cost(heads, keys):
    flops = 4 * BLOCK_QUERIES * heads * keys * HEAD_SIZE
    return pl.CostEstimate(flops=flops, bytes_accessed=2 * 2**20, transcendentals=flops // 512)


smem = pl.BlockSpec(memory_space=pltpu.SMEM)
vmem = pl.BlockSpec(memory_space=pltpu.VMEM)
anywhere = pl.BlockSpec(memory_space=pl.ANY)
small = pltpu.CompilerParams(vmem_limit_bytes=4 * 2**20)
params = pltpu.CompilerParams(vmem_limit_bytes=24 * 2**20)
slight = pl.CostEstimate(flops=1000, bytes_accessed=1000, transcendentals=0)


def wide_shapes(count):
    return (jax.ShapeDtypeStruct((HEAD_SIZE, count), jnp.bfloat16),
            jax.ShapeDtypeStruct((count, 2 * HEAD_SIZE), jnp.bfloat16))


def cut(queries, after):
    rows, width = queries.shape
    return pl.pallas_call(
        cut_kernel,
        out_shape=jax.ShapeDtypeStruct((KEY_HEADS, rows, width // KEY_HEADS), jnp.bfloat16),
        in_specs=[vmem, anywhere],
        out_specs=vmem,
        compiler_params=small,
        cost_estimate=slight,
        name="cut",
    )(queries, after)


def choose(shift, facts, moved, held, after, estimate):
    return pl.pallas_call(
        functools.partial(choose_kernel, shift),
        out_shape=jax.ShapeDtypeStruct(held.shape, held.dtype),
        in_specs=[vmem, vmem, vmem, anywhere],
        out_specs=vmem,
        compiler_params=small,
        cost_estimate=estimate,
        name="choose",
    )(facts, moved, held, after)


def widen(kv, after):
    return pl.pallas_call(
        widen_kernel,
        out_shape=wide_shapes(CACHE_SLOTS),
        in_specs=[vmem, anywhere],
        out_specs=(vmem, vmem),
        compiler_params=params,
        cost_estimate=cost(GROUP, CACHE_SLOTS),
        name="widen",
    )(kv, after)


def attend_local(facts, q, keys, vals):
    return pl.pallas_call(
        local_kernel,
        out_shape=jax.ShapeDtypeStruct((GROUP, BLOCK_QUERIES, 2 * HEAD_SIZE), jnp.float32),
        in_specs=[vmem] * 4,
        out_specs=vmem,
        scratch_shapes=[pltpu.VMEM((2, STACK * BLOCK_QUERIES, CACHE_SLOTS), jnp.bfloat16)],
        compiler_params=params,
        cost_estimate=cost(GROUP, CACHE_SLOTS),
        name="attend_local",
    )(facts, q, keys, vals)


def attend_anchor(facts, moved, held, q, keys, vals, states):
    return pl.pallas_call(
        anchor_kernel,
        out_shape=jax.ShapeDtypeStruct(q.shape, jnp.bfloat16),
        in_specs=[vmem] * 7,
        out_specs=vmem,
        scratch_shapes=[
            pltpu.VMEM(held.shape, held.dtype),
            *(pltpu.VMEM(wide.shape, wide.dtype) for wide in wide_shapes(ANCHOR_SLOTS)),
            pltpu.VMEM((GROUP // STACK, STACK * BLOCK_QUERIES, ANCHOR_SLOTS), jnp.bfloat16),
            pltpu.VMEM((BLOCK_QUERIES, ANCHOR_SLOTS + CACHE_SLOTS), jnp.float32),
        ],
        compiler_params=params,
        cost_estimate=cost(GROUP, ANCHOR_SLOTS),
        name="attend_anchor",
    )(facts, moved, held, q, keys, vals, states)


def body(queries, kv_cache, anchor_src, stretch_pos):
    block = lax.axis_index("ctx").astype(jnp.int32)
    blocks = lax.axis_size("ctx")
    which = lax.broadcasted_iota(jnp.int32, (2, 8, 128), 0)
    facts = jnp.where(which == 0, stretch_pos.reshape(1, 1, 1) // TILE, block - anchor_src.reshape(1, 1, 1))
    held = lax.optimization_barrier(kv_cache[:, :ANCHOR_SLOTS, :])

    def from_earlier(held, shift):
        return lax.ppermute(held, "ctx", [(b, b + shift) for b in range(blocks - shift)])

    moved = from_earlier(held, 2)
    q = lax.all_to_all(cut(queries, held), "head", split_axis=0, concat_axis=0, tiled=True)
    q = q.reshape(BLOCK_QUERIES, GROUP * HEAD_SIZE)
    held = choose(2, facts, moved, held, facts, cost(GROUP, CACHE_SLOTS))
    moved = from_earlier(held, 4)
    keys, vals = widen(kv_cache, held)
    held = choose(4, facts, moved, held, keys, slight)
    moved = from_earlier(held, 1)
    states = attend_local(facts, q, keys, vals)
    result = attend_anchor(facts, moved, held, q, keys, vals, states)
    return lax.all_to_all(result, "head", split_axis=0, concat_axis=1, tiled=True)


def solution(mesh):
    in_specs = (P(("ctx", "head"), None), P(None, "ctx", "head"), P("ctx"), P("ctx"))
    out_specs = P(("ctx", "head"), None)
    return jax.shard_map(body, mesh=mesh, in_specs=in_specs, out_specs=out_specs, check_vma=False)
```

```python
import functools
import math

import jax
import jax.numpy as jnp
from jax import lax
from jax.experimental import pallas as pl
from jax.experimental.pallas import tpu as pltpu
from jax.sharding import PartitionSpec as P

QUERY_HEAD_COUNT = 64
KEY_HEADS = 8
HEAD_SIZE = 128
GROUP = QUERY_HEAD_COUNT // KEY_HEADS
BLOCK_QUERIES = 256
CACHE_SLOTS = 2048
ANCHOR_SLOTS = 512
SPAN = 8
TILE = 256
FIRST_HEADS = 4
STACK = 2
CHUNK = 512

masked_score = -1e30
EXP2_SCALE = math.log2(math.e) / math.sqrt(HEAD_SIZE)
SAFE_LOW, SAFE_HIGH = 2.0**-60, 2.0**60


def head_columns(g):
    return slice(g * HEAD_SIZE, (g + 1) * HEAD_SIZE)


def cut_kernel(queries, after, outgoing):
    pieces, _, width = outgoing.shape
    for h in range(pieces):
        outgoing[h] = queries[:, h * width:(h + 1) * width]


def full_tiles_of(facts):
    return jnp.max(facts[0])


def place_of(facts):
    return jnp.max(facts[1])


def choose_kernel(shift, facts, moved, held, after, out):
    arrived = (place_of(facts) & shift) != 0

    @pl.when(arrived)
    def _():
        out[...] = moved[...]

    @pl.when(jnp.logical_not(arrived))
    def _():
        out[...] = held[...]


def widen_kernel(part_ref, after, keys, vals):
    widen_into(part_ref, keys, vals)


def widen_into(part_ref, keys, vals):
    keys[...] = part_ref[0].astype(jnp.float32).T.astype(jnp.bfloat16)
    vals[:, 0:HEAD_SIZE] = part_ref[1]
    vals[:, HEAD_SIZE:] = jnp.ones(part_ref.shape[1:], jnp.bfloat16)


def scaled_scores(q, keys):
    return jnp.dot(q, keys, preferred_element_type=jnp.float32) * EXP2_SCALE


def stacked(q_ref, first):
    return jnp.concatenate([q_ref[:, head_columns(first + g)] for g in range(STACK)], axis=0)


def rows_of(g):
    return slice(g * BLOCK_QUERIES, (g + 1) * BLOCK_QUERIES)


def tile_of(tile):
    return slice(tile * TILE, (tile + 1) * TILE)


def tile_at(tile):
    return pl.ds(pl.multiple_of(tile * TILE, TILE), TILE)


def causal_slant():
    row = lax.broadcasted_iota(jnp.int32, (BLOCK_QUERIES, TILE), 0)
    col = lax.broadcasted_iota(jnp.int32, (BLOCK_QUERIES, TILE), 1)
    return col - row


def local_kernel(first, facts, q_ref, keys, vals, state_ref, weights):
    stacks = state_ref.shape[0] // STACK
    full_tiles = full_tiles_of(facts)
    slant = causal_slant()

    def attend(chunks):
        span = chunks * CHUNK
        tiles = span // TILE

        def weigh(stack):
            q = stacked(q_ref, first + stack * STACK)
            for tile in range(tiles):
                s = scaled_scores(q, keys[:, tile_of(tile)])
                if tile * TILE >= span - CHUNK:
                    allowed = slant <= (full_tiles - tile) * TILE
                    s = jnp.where(jnp.concatenate([allowed] * STACK, axis=0), s, masked_score)
                weights[stack % 2, :, tile_of(tile)] = jnp.exp2(s).astype(jnp.bfloat16)

        weigh(0)
        for stack in range(stacks):
            if stack + 1 < stacks:
                weigh(stack + 1)
            mixed = jnp.dot(weights[stack % 2, :, 0:span], vals[0:span, :], preferred_element_type=jnp.float32)
            for g in range(STACK):
                state_ref[stack * STACK + g] = mixed[rows_of(g)]

    for chunks in range(1, CACHE_SLOTS // CHUNK + 1):
        pl.when(full_tiles * TILE // CHUNK == chunks - 1)(functools.partial(attend, chunks))


def exact_head(g, full_tiles, has_anchor, q_ref, local, anchor, scores):
    q = q_ref[:, head_columns(g)]
    slant = causal_slant()
    base = ANCHOR_SLOTS // TILE
    zero = jnp.zeros((BLOCK_QUERIES, 2 * HEAD_SIZE), jnp.float32)

    def score_into(slot, keys, tile, allowed, peak):
        s = jnp.where(allowed, scaled_scores(q, keys[:, tile_at(tile)]), masked_score)
        scores[:, tile_at(slot + tile)] = s
        return jnp.maximum(peak, jnp.max(s, axis=1, keepdims=True))

    def mix_from(slot, vals, tile, mixed):
        p = jnp.exp2(scores[:, tile_at(slot + tile)] - peak).astype(jnp.bfloat16)
        return mixed + jnp.dot(p, vals[tile_at(tile), :], preferred_element_type=jnp.float32)

    peak = jnp.full((BLOCK_QUERIES, 1), masked_score, jnp.float32)
    peak = lax.fori_loop(
        0, full_tiles + 1,
        lambda tile, peak: score_into(base, local[0], tile, slant <= (full_tiles - tile) * TILE, peak), peak)
    peak = lax.fori_loop(
        0, base, lambda tile, peak: score_into(0, anchor[0], tile, jnp.logical_and(has_anchor, slant == slant), peak),
        peak)
    mixed = lax.fori_loop(0, full_tiles + 1, functools.partial(mix_from, base, local[1]), zero)
    return lax.fori_loop(0, base, functools.partial(mix_from, 0, anchor[1]), mixed)


def anchor_kernel(facts, moved, held, q_ref, local_keys, local_vals, early, late, out_ref,
                  anchor, keys, vals, weights, scores):
    states = [part.at[g] for part in (early, late) for g in range(part.shape[0])]
    heads = len(states)
    has_anchor = place_of(facts) > 0
    choose_kernel(1, facts, moved, held, None, anchor)
    widen_into(anchor, keys, vals)

    def write(g, mixed):
        out_ref[:, head_columns(g)] = (mixed[:, :HEAD_SIZE] / mixed[:, HEAD_SIZE:]).astype(jnp.bfloat16)

    for stack in range(heads // STACK):
        s = jnp.where(has_anchor, scaled_scores(stacked(q_ref, stack * STACK), keys[...]), masked_score)
        weights[stack] = jnp.exp2(s).astype(jnp.bfloat16)
    low = high = None
    for stack in range(heads // STACK):
        both = jnp.dot(weights[stack], vals[...], preferred_element_type=jnp.float32)
        for g in range(STACK):
            state = states[stack * STACK + g][...]
            mixed = both[rows_of(g)] + state
            write(stack * STACK + g, mixed)
            below, above = state[:, HEAD_SIZE:], mixed[:, HEAD_SIZE:]
            low = below if low is None else jnp.minimum(low, below)
            high = above if high is None else jnp.maximum(high, above)
    safe = jnp.logical_and(jnp.min(low) > SAFE_LOW, jnp.max(high) < SAFE_HIGH)

    @pl.when(jnp.logical_not(safe))
    def _():
        for g in range(heads):
            write(g, exact_head(g, full_tiles_of(facts), has_anchor, q_ref, (local_keys, local_vals), (keys, vals), scores))


def cost(heads, keys):
    flops = 4 * BLOCK_QUERIES * heads * keys * HEAD_SIZE
    return pl.CostEstimate(flops=flops, bytes_accessed=2 * 2**20, transcendentals=flops // 512)


smem = pl.BlockSpec(memory_space=pltpu.SMEM)
vmem = pl.BlockSpec(memory_space=pltpu.VMEM)
anywhere = pl.BlockSpec(memory_space=pl.ANY)
small = pltpu.CompilerParams(vmem_limit_bytes=4 * 2**20)
params = pltpu.CompilerParams(vmem_limit_bytes=24 * 2**20)
slight = pl.CostEstimate(flops=1000, bytes_accessed=1000, transcendentals=0)


def wide_shapes(count):
    return (jax.ShapeDtypeStruct((HEAD_SIZE, count), jnp.bfloat16),
            jax.ShapeDtypeStruct((count, 2 * HEAD_SIZE), jnp.bfloat16))


def cut(queries, after):
    rows, width = queries.shape
    return pl.pallas_call(
        cut_kernel,
        out_shape=jax.ShapeDtypeStruct((KEY_HEADS, rows, width // KEY_HEADS), jnp.bfloat16),
        in_specs=[vmem, anywhere],
        out_specs=vmem,
        compiler_params=small,
        cost_estimate=slight,
        name="cut",
    )(queries, after)


def choose(shift, facts, moved, held, after, estimate):
    return pl.pallas_call(
        functools.partial(choose_kernel, shift),
        out_shape=jax.ShapeDtypeStruct(held.shape, held.dtype),
        in_specs=[vmem, vmem, vmem, anywhere],
        out_specs=vmem,
        compiler_params=small,
        cost_estimate=estimate,
        name="choose",
    )(facts, moved, held, after)


def widen(kv, after):
    return pl.pallas_call(
        widen_kernel,
        out_shape=wide_shapes(CACHE_SLOTS),
        in_specs=[vmem, anywhere],
        out_specs=(vmem, vmem),
        compiler_params=params,
        cost_estimate=cost(GROUP, CACHE_SLOTS),
        name="widen",
    )(kv, after)


def attend_local(first, heads, facts, q, keys, vals):
    return pl.pallas_call(
        functools.partial(local_kernel, first),
        out_shape=jax.ShapeDtypeStruct((heads, BLOCK_QUERIES, 2 * HEAD_SIZE), jnp.float32),
        in_specs=[vmem] * 4,
        out_specs=vmem,
        scratch_shapes=[pltpu.VMEM((2, STACK * BLOCK_QUERIES, CACHE_SLOTS), jnp.bfloat16)],
        compiler_params=params,
        cost_estimate=cost(GROUP, CACHE_SLOTS),
        name="attend_local",
    )(facts, q, keys, vals)


def attend_anchor(facts, moved, held, q, keys, vals, early, late):
    return pl.pallas_call(
        anchor_kernel,
        out_shape=jax.ShapeDtypeStruct(q.shape, jnp.bfloat16),
        in_specs=[vmem] * 8,
        out_specs=vmem,
        scratch_shapes=[
            pltpu.VMEM(held.shape, held.dtype),
            *(pltpu.VMEM(wide.shape, wide.dtype) for wide in wide_shapes(ANCHOR_SLOTS)),
            pltpu.VMEM((GROUP // STACK, STACK * BLOCK_QUERIES, ANCHOR_SLOTS), jnp.bfloat16),
            pltpu.VMEM((BLOCK_QUERIES, ANCHOR_SLOTS + CACHE_SLOTS), jnp.float32),
        ],
        compiler_params=params,
        cost_estimate=cost(GROUP, ANCHOR_SLOTS),
        name="attend_anchor",
    )(facts, moved, held, q, keys, vals, early, late)


def body(queries, kv_cache, anchor_src, stretch_pos):
    block = lax.axis_index("ctx").astype(jnp.int32)
    blocks = lax.axis_size("ctx")
    which = lax.broadcasted_iota(jnp.int32, (2, 8, 128), 0)
    facts = jnp.where(which == 0, stretch_pos.reshape(1, 1, 1) // TILE, block - anchor_src.reshape(1, 1, 1))
    held = lax.optimization_barrier(kv_cache[:, :ANCHOR_SLOTS, :])

    def from_earlier(held, shift):
        return lax.ppermute(held, "ctx", [(b, b + shift) for b in range(blocks - shift)])

    moved = from_earlier(held, 2)
    q = lax.all_to_all(cut(queries, held), "head", split_axis=0, concat_axis=0, tiled=True)
    q = q.reshape(BLOCK_QUERIES, GROUP * HEAD_SIZE)
    held = choose(2, facts, moved, held, facts, cost(GROUP, CACHE_SLOTS))
    moved = from_earlier(held, 4)
    keys, vals = widen(kv_cache, held)
    held = choose(4, facts, moved, held, keys, slight)
    early = attend_local(0, FIRST_HEADS, facts, q, keys, vals)
    held, early = lax.optimization_barrier((held, early))
    moved = from_earlier(held, 1)
    late = attend_local(FIRST_HEADS, GROUP - FIRST_HEADS, facts, q, keys, vals)
    result = attend_anchor(facts, moved, held, q, keys, vals, early, late)
    return lax.all_to_all(result, "head", split_axis=0, concat_axis=1, tiled=True)


def solution(mesh):
    in_specs = (P(("ctx", "head"), None), P(None, "ctx", "head"), P("ctx"), P("ctx"))
    out_specs = P(("ctx", "head"), None)
    return jax.shard_map(body, mesh=mesh, in_specs=in_specs, out_specs=out_specs, check_vma=False)
```

```python
import functools
import math

import jax
import jax.numpy as jnp
from jax import lax
from jax.experimental import pallas as pl
from jax.experimental.pallas import tpu as pltpu
from jax.sharding import PartitionSpec as P

QUERY_HEAD_COUNT = 64
KEY_HEADS = 8
HEAD_SIZE = 128
GROUP = QUERY_HEAD_COUNT // KEY_HEADS
BLOCK_QUERIES = 256
CACHE_SLOTS = 2048
ANCHOR_SLOTS = 512
SPAN = 8
TILE = 256
FIRST_HEADS = 4
STACK = 2
CHUNK = 512

masked_score = -1e30
EXP2_SCALE = math.log2(math.e) / math.sqrt(HEAD_SIZE)
SAFE_LOW, SAFE_HIGH = 2.0**-60, 2.0**60


def head_columns(g):
    return slice(g * HEAD_SIZE, (g + 1) * HEAD_SIZE)


def cut_kernel(queries, after, outgoing):
    pieces, _, width = outgoing.shape
    for h in range(pieces):
        outgoing[h] = queries[:, h * width:(h + 1) * width]


def full_tiles_of(facts):
    return jnp.max(facts[0])


def place_of(facts):
    return jnp.max(facts[1])


def choose_kernel(shift, facts, moved, held, after, out):
    arrived = (place_of(facts) & shift) != 0

    @pl.when(arrived)
    def _():
        out[...] = moved[...]

    @pl.when(jnp.logical_not(arrived))
    def _():
        out[...] = held[...]


def widen_kernel(part_ref, after, keys, vals):
    widen_into(part_ref, keys, vals)


def widen_into(part_ref, keys, vals):
    keys[...] = part_ref[0].astype(jnp.float32).T.astype(jnp.bfloat16)
    vals[:, 0:HEAD_SIZE] = part_ref[1]
    vals[:, HEAD_SIZE:] = jnp.ones(part_ref.shape[1:], jnp.bfloat16)


def scaled_scores(q, keys):
    return jnp.dot(q, keys, preferred_element_type=jnp.float32) * EXP2_SCALE


def stacked(q_ref, first):
    return jnp.concatenate([q_ref[:, head_columns(first + g)] for g in range(STACK)], axis=0)


def rows_of(g):
    return slice(g * BLOCK_QUERIES, (g + 1) * BLOCK_QUERIES)


def tile_of(tile):
    return slice(tile * TILE, (tile + 1) * TILE)


def tile_at(tile):
    return pl.ds(pl.multiple_of(tile * TILE, TILE), TILE)


def causal_slant():
    row = lax.broadcasted_iota(jnp.int32, (BLOCK_QUERIES, TILE), 0)
    col = lax.broadcasted_iota(jnp.int32, (BLOCK_QUERIES, TILE), 1)
    return col - row


def local_kernel(first, facts, q_ref, keys, vals, state_ref, weights):
    stacks = state_ref.shape[0] // STACK
    full_tiles = full_tiles_of(facts)
    slant = causal_slant()

    def attend(chunks):
        span = chunks * CHUNK
        tiles = span // TILE

        def weigh(stack):
            q = stacked(q_ref, first + stack * STACK)
            for tile in range(tiles):
                s = scaled_scores(q, keys[:, tile_of(tile)])
                if tile * TILE >= span - CHUNK:
                    allowed = slant <= (full_tiles - tile) * TILE
                    s = jnp.where(jnp.concatenate([allowed] * STACK, axis=0), s, masked_score)
                weights[stack % 2, :, tile_of(tile)] = jnp.exp2(s).astype(jnp.bfloat16)

        weigh(0)
        for stack in range(stacks):
            if stack + 1 < stacks:
                weigh(stack + 1)
            mixed = jnp.dot(weights[stack % 2, :, 0:span], vals[0:span, :], preferred_element_type=jnp.float32)
            for g in range(STACK):
                state_ref[stack * STACK + g] = mixed[rows_of(g)]

    for chunks in range(1, CACHE_SLOTS // CHUNK + 1):
        pl.when(full_tiles * TILE // CHUNK == chunks - 1)(functools.partial(attend, chunks))


def exact_head(g, full_tiles, has_anchor, q_ref, local, anchor, scores):
    q = q_ref[:, head_columns(g)]
    slant = causal_slant()
    base = ANCHOR_SLOTS // TILE
    zero = jnp.zeros((BLOCK_QUERIES, 2 * HEAD_SIZE), jnp.float32)

    def score_into(slot, keys, tile, allowed, peak):
        s = jnp.where(allowed, scaled_scores(q, keys[:, tile_at(tile)]), masked_score)
        scores[:, tile_at(slot + tile)] = s
        return jnp.maximum(peak, jnp.max(s, axis=1, keepdims=True))

    def mix_from(slot, vals, tile, mixed):
        p = jnp.exp2(scores[:, tile_at(slot + tile)] - peak).astype(jnp.bfloat16)
        return mixed + jnp.dot(p, vals[tile_at(tile), :], preferred_element_type=jnp.float32)

    peak = jnp.full((BLOCK_QUERIES, 1), masked_score, jnp.float32)
    peak = lax.fori_loop(
        0, full_tiles + 1,
        lambda tile, peak: score_into(base, local[0], tile, slant <= (full_tiles - tile) * TILE, peak), peak)
    peak = lax.fori_loop(
        0, base, lambda tile, peak: score_into(0, anchor[0], tile, jnp.logical_and(has_anchor, slant == slant), peak),
        peak)
    mixed = lax.fori_loop(0, full_tiles + 1, functools.partial(mix_from, base, local[1]), zero)
    return lax.fori_loop(0, base, functools.partial(mix_from, 0, anchor[1]), mixed)


def anchor_kernel(facts, moved, held, q_ref, local_keys, local_vals, early, late, out_ref,
                  anchor, keys, vals, weights, scores):
    states = [part.at[g] for part in (early, late) for g in range(part.shape[0])]
    heads = len(states)
    has_anchor = place_of(facts) > 0
    choose_kernel(4, facts, moved, held, None, anchor)
    widen_into(anchor, keys, vals)

    def write(g, mixed):
        out_ref[:, head_columns(g)] = (mixed[:, :HEAD_SIZE] / mixed[:, HEAD_SIZE:]).astype(jnp.bfloat16)

    for stack in range(heads // STACK):
        s = jnp.where(has_anchor, scaled_scores(stacked(q_ref, stack * STACK), keys[...]), masked_score)
        weights[stack] = jnp.exp2(s).astype(jnp.bfloat16)
    low = high = None
    for stack in range(heads // STACK):
        both = jnp.dot(weights[stack], vals[...], preferred_element_type=jnp.float32)
        for g in range(STACK):
            state = states[stack * STACK + g][...]
            mixed = both[rows_of(g)] + state
            write(stack * STACK + g, mixed)
            below, above = state[:, HEAD_SIZE:], mixed[:, HEAD_SIZE:]
            low = below if low is None else jnp.minimum(low, below)
            high = above if high is None else jnp.maximum(high, above)
    safe = jnp.logical_and(jnp.min(low) > SAFE_LOW, jnp.max(high) < SAFE_HIGH)

    @pl.when(jnp.logical_not(safe))
    def _():
        for g in range(heads):
            write(g, exact_head(g, full_tiles_of(facts), has_anchor, q_ref, (local_keys, local_vals), (keys, vals), scores))


def cost(heads, keys):
    flops = 4 * BLOCK_QUERIES * heads * keys * HEAD_SIZE
    return pl.CostEstimate(flops=flops, bytes_accessed=2 * 2**20, transcendentals=flops // 512)


smem = pl.BlockSpec(memory_space=pltpu.SMEM)
vmem = pl.BlockSpec(memory_space=pltpu.VMEM)
anywhere = pl.BlockSpec(memory_space=pl.ANY)
small = pltpu.CompilerParams(vmem_limit_bytes=4 * 2**20)
params = pltpu.CompilerParams(vmem_limit_bytes=24 * 2**20)
slight = pl.CostEstimate(flops=1000, bytes_accessed=1000, transcendentals=0)


def wide_shapes(count):
    return (jax.ShapeDtypeStruct((HEAD_SIZE, count), jnp.bfloat16),
            jax.ShapeDtypeStruct((count, 2 * HEAD_SIZE), jnp.bfloat16))


def cut(queries, after):
    rows, width = queries.shape
    return pl.pallas_call(
        cut_kernel,
        out_shape=jax.ShapeDtypeStruct((KEY_HEADS, rows, width // KEY_HEADS), jnp.bfloat16),
        in_specs=[vmem, anywhere],
        out_specs=vmem,
        compiler_params=small,
        cost_estimate=slight,
        name="cut",
    )(queries, after)


def choose(shift, facts, moved, held, after, estimate):
    return pl.pallas_call(
        functools.partial(choose_kernel, shift),
        out_shape=jax.ShapeDtypeStruct(held.shape, held.dtype),
        in_specs=[vmem, vmem, vmem, anywhere],
        out_specs=vmem,
        compiler_params=small,
        cost_estimate=estimate,
        name="choose",
    )(facts, moved, held, after)


def widen(kv, after):
    return pl.pallas_call(
        widen_kernel,
        out_shape=wide_shapes(CACHE_SLOTS),
        in_specs=[vmem, anywhere],
        out_specs=(vmem, vmem),
        compiler_params=params,
        cost_estimate=cost(GROUP, CACHE_SLOTS),
        name="widen",
    )(kv, after)


def attend_local(first, heads, facts, q, keys, vals):
    return pl.pallas_call(
        functools.partial(local_kernel, first),
        out_shape=jax.ShapeDtypeStruct((heads, BLOCK_QUERIES, 2 * HEAD_SIZE), jnp.float32),
        in_specs=[vmem] * 4,
        out_specs=vmem,
        scratch_shapes=[pltpu.VMEM((2, STACK * BLOCK_QUERIES, CACHE_SLOTS), jnp.bfloat16)],
        compiler_params=params,
        cost_estimate=cost(GROUP, CACHE_SLOTS),
        name="attend_local",
    )(facts, q, keys, vals)


def attend_anchor(facts, moved, held, q, keys, vals, early, late):
    return pl.pallas_call(
        anchor_kernel,
        out_shape=jax.ShapeDtypeStruct(q.shape, jnp.bfloat16),
        in_specs=[vmem] * 8,
        out_specs=vmem,
        scratch_shapes=[
            pltpu.VMEM(held.shape, held.dtype),
            *(pltpu.VMEM(wide.shape, wide.dtype) for wide in wide_shapes(ANCHOR_SLOTS)),
            pltpu.VMEM((GROUP // STACK, STACK * BLOCK_QUERIES, ANCHOR_SLOTS), jnp.bfloat16),
            pltpu.VMEM((BLOCK_QUERIES, ANCHOR_SLOTS + CACHE_SLOTS), jnp.float32),
        ],
        compiler_params=params,
        cost_estimate=cost(GROUP, ANCHOR_SLOTS),
        name="attend_anchor",
    )(facts, moved, held, q, keys, vals, early, late)


def body(queries, kv_cache, anchor_src, stretch_pos):
    block = lax.axis_index("ctx").astype(jnp.int32)
    blocks = lax.axis_size("ctx")
    which = lax.broadcasted_iota(jnp.int32, (2, 8, 128), 0)
    facts = jnp.where(which == 0, stretch_pos.reshape(1, 1, 1) // TILE, block - anchor_src.reshape(1, 1, 1))
    held = lax.optimization_barrier(kv_cache[:, :ANCHOR_SLOTS, :])

    def from_earlier(held, shift):
        return lax.ppermute(held, "ctx", [(b, b + shift) for b in range(blocks - shift)])

    moved = from_earlier(held, 2)
    q = lax.all_to_all(cut(queries, held), "head", split_axis=0, concat_axis=0, tiled=True)
    q = q.reshape(BLOCK_QUERIES, GROUP * HEAD_SIZE)
    held = choose(2, facts, moved, held, facts, cost(GROUP, CACHE_SLOTS))
    moved = from_earlier(held, 1)
    keys, vals = widen(kv_cache, held)
    held = choose(1, facts, moved, held, keys, slight)
    early = attend_local(0, FIRST_HEADS, facts, q, keys, vals)
    held, early = lax.optimization_barrier((held, early))
    moved = from_earlier(held, 4)
    late = attend_local(FIRST_HEADS, GROUP - FIRST_HEADS, facts, q, keys, vals)
    result = attend_anchor(facts, moved, held, q, keys, vals, early, late)
    return lax.all_to_all(result, "head", split_axis=0, concat_axis=1, tiled=True)


def solution(mesh):
    in_specs = (P(("ctx", "head"), None), P(None, "ctx", "head"), P("ctx"), P("ctx"))
    out_specs = P(("ctx", "head"), None)
    return jax.shard_map(body, mesh=mesh, in_specs=in_specs, out_specs=out_specs, check_vma=False)
```

```python
import functools
import math

import jax
import jax.numpy as jnp
from jax import lax
from jax.experimental import pallas as pl
from jax.experimental.pallas import tpu as pltpu
from jax.sharding import PartitionSpec as P

QUERY_HEAD_COUNT = 64
KEY_HEADS = 8
HEAD_SIZE = 128
GROUP = QUERY_HEAD_COUNT // KEY_HEADS
BLOCK_QUERIES = 256
CACHE_SLOTS = 2048
ANCHOR_SLOTS = 512
SPAN = 8
TILE = 256
FIRST_HEADS = 2
STACK = 2
CHUNK = 512

masked_score = -1e30
EXP2_SCALE = math.log2(math.e) / math.sqrt(HEAD_SIZE)
SAFE_LOW, SAFE_HIGH = 2.0**-60, 2.0**60


def head_columns(g):
    return slice(g * HEAD_SIZE, (g + 1) * HEAD_SIZE)


def cut_kernel(queries, after, outgoing):
    pieces, _, width = outgoing.shape
    for h in range(pieces):
        outgoing[h] = queries[:, h * width:(h + 1) * width]


def full_tiles_of(facts):
    return jnp.max(facts[0])


def place_of(facts):
    return jnp.max(facts[1])


def choose_kernel(shift, facts, moved, held, after, out):
    arrived = (place_of(facts) & shift) != 0

    @pl.when(arrived)
    def _():
        out[...] = moved[...]

    @pl.when(jnp.logical_not(arrived))
    def _():
        out[...] = held[...]


def widen_kernel(part_ref, after, keys, vals):
    widen_into(part_ref, keys, vals)


def widen_into(part_ref, keys, vals):
    keys[...] = part_ref[0].astype(jnp.float32).T.astype(jnp.bfloat16)
    vals[:, 0:HEAD_SIZE] = part_ref[1]
    vals[:, HEAD_SIZE:] = jnp.ones(part_ref.shape[1:], jnp.bfloat16)


def scaled_scores(q, keys):
    return jnp.dot(q, keys, preferred_element_type=jnp.float32) * EXP2_SCALE


def stacked(q_ref, first):
    return jnp.concatenate([q_ref[:, head_columns(first + g)] for g in range(STACK)], axis=0)


def rows_of(g):
    return slice(g * BLOCK_QUERIES, (g + 1) * BLOCK_QUERIES)


def tile_of(tile):
    return slice(tile * TILE, (tile + 1) * TILE)


def tile_at(tile):
    return pl.ds(pl.multiple_of(tile * TILE, TILE), TILE)


def causal_slant():
    row = lax.broadcasted_iota(jnp.int32, (BLOCK_QUERIES, TILE), 0)
    col = lax.broadcasted_iota(jnp.int32, (BLOCK_QUERIES, TILE), 1)
    return col - row


def local_kernel(first, facts, q_ref, keys, vals, state_ref, weights):
    stacks = state_ref.shape[0] // STACK
    full_tiles = full_tiles_of(facts)
    slant = causal_slant()

    def attend(chunks):
        span = chunks * CHUNK
        tiles = span // TILE

        def weigh(stack):
            q = stacked(q_ref, first + stack * STACK)
            for tile in range(tiles):
                s = scaled_scores(q, keys[:, tile_of(tile)])
                if tile * TILE >= span - CHUNK:
                    allowed = slant <= (full_tiles - tile) * TILE
                    s = jnp.where(jnp.concatenate([allowed] * STACK, axis=0), s, masked_score)
                weights[stack % 2, :, tile_of(tile)] = jnp.exp2(s).astype(jnp.bfloat16)

        weigh(0)
        for stack in range(stacks):
            if stack + 1 < stacks:
                weigh(stack + 1)
            mixed = jnp.dot(weights[stack % 2, :, 0:span], vals[0:span, :], preferred_element_type=jnp.float32)
            for g in range(STACK):
                state_ref[stack * STACK + g] = mixed[rows_of(g)]

    for chunks in range(1, CACHE_SLOTS // CHUNK + 1):
        pl.when(full_tiles * TILE // CHUNK == chunks - 1)(functools.partial(attend, chunks))


def exact_head(g, full_tiles, has_anchor, q_ref, local, anchor, scores):
    q = q_ref[:, head_columns(g)]
    slant = causal_slant()
    base = ANCHOR_SLOTS // TILE
    zero = jnp.zeros((BLOCK_QUERIES, 2 * HEAD_SIZE), jnp.float32)

    def score_into(slot, keys, tile, allowed, peak):
        s = jnp.where(allowed, scaled_scores(q, keys[:, tile_at(tile)]), masked_score)
        scores[:, tile_at(slot + tile)] = s
        return jnp.maximum(peak, jnp.max(s, axis=1, keepdims=True))

    def mix_from(slot, vals, tile, mixed):
        p = jnp.exp2(scores[:, tile_at(slot + tile)] - peak).astype(jnp.bfloat16)
        return mixed + jnp.dot(p, vals[tile_at(tile), :], preferred_element_type=jnp.float32)

    peak = jnp.full((BLOCK_QUERIES, 1), masked_score, jnp.float32)
    peak = lax.fori_loop(
        0, full_tiles + 1,
        lambda tile, peak: score_into(base, local[0], tile, slant <= (full_tiles - tile) * TILE, peak), peak)
    peak = lax.fori_loop(
        0, base, lambda tile, peak: score_into(0, anchor[0], tile, jnp.logical_and(has_anchor, slant == slant), peak),
        peak)
    mixed = lax.fori_loop(0, full_tiles + 1, functools.partial(mix_from, base, local[1]), zero)
    return lax.fori_loop(0, base, functools.partial(mix_from, 0, anchor[1]), mixed)


def anchor_kernel(facts, moved, held, q_ref, local_keys, local_vals, early, late, out_ref,
                  anchor, keys, vals, weights, scores):
    states = [part.at[g] for part in (early, late) for g in range(part.shape[0])]
    heads = len(states)
    has_anchor = place_of(facts) > 0
    choose_kernel(4, facts, moved, held, None, anchor)
    widen_into(anchor, keys, vals)

    def write(g, mixed):
        out_ref[:, head_columns(g)] = (mixed[:, :HEAD_SIZE] / mixed[:, HEAD_SIZE:]).astype(jnp.bfloat16)

    for stack in range(heads // STACK):
        s = jnp.where(has_anchor, scaled_scores(stacked(q_ref, stack * STACK), keys[...]), masked_score)
        weights[stack] = jnp.exp2(s).astype(jnp.bfloat16)
    low = high = None
    for stack in range(heads // STACK):
        both = jnp.dot(weights[stack], vals[...], preferred_element_type=jnp.float32)
        for g in range(STACK):
            state = states[stack * STACK + g][...]
            mixed = both[rows_of(g)] + state
            write(stack * STACK + g, mixed)
            below, above = state[:, HEAD_SIZE:], mixed[:, HEAD_SIZE:]
            low = below if low is None else jnp.minimum(low, below)
            high = above if high is None else jnp.maximum(high, above)
    safe = jnp.logical_and(jnp.min(low) > SAFE_LOW, jnp.max(high) < SAFE_HIGH)

    @pl.when(jnp.logical_not(safe))
    def _():
        for g in range(heads):
            write(g, exact_head(g, full_tiles_of(facts), has_anchor, q_ref, (local_keys, local_vals), (keys, vals), scores))


def cost(heads, keys):
    flops = 4 * BLOCK_QUERIES * heads * keys * HEAD_SIZE
    return pl.CostEstimate(flops=flops, bytes_accessed=2 * 2**20, transcendentals=flops // 512)


smem = pl.BlockSpec(memory_space=pltpu.SMEM)
vmem = pl.BlockSpec(memory_space=pltpu.VMEM)
anywhere = pl.BlockSpec(memory_space=pl.ANY)
small = pltpu.CompilerParams(vmem_limit_bytes=4 * 2**20)
params = pltpu.CompilerParams(vmem_limit_bytes=24 * 2**20)
slight = pl.CostEstimate(flops=1000, bytes_accessed=1000, transcendentals=0)


def wide_shapes(count):
    return (jax.ShapeDtypeStruct((HEAD_SIZE, count), jnp.bfloat16),
            jax.ShapeDtypeStruct((count, 2 * HEAD_SIZE), jnp.bfloat16))


def cut(queries, after):
    rows, width = queries.shape
    return pl.pallas_call(
        cut_kernel,
        out_shape=jax.ShapeDtypeStruct((KEY_HEADS, rows, width // KEY_HEADS), jnp.bfloat16),
        in_specs=[vmem, anywhere],
        out_specs=vmem,
        compiler_params=small,
        cost_estimate=slight,
        name="cut",
    )(queries, after)


def choose(shift, facts, moved, held, after, estimate):
    return pl.pallas_call(
        functools.partial(choose_kernel, shift),
        out_shape=jax.ShapeDtypeStruct(held.shape, held.dtype),
        in_specs=[vmem, vmem, vmem, anywhere],
        out_specs=vmem,
        compiler_params=small,
        cost_estimate=estimate,
        name="choose",
    )(facts, moved, held, after)


def widen(kv, after):
    return pl.pallas_call(
        widen_kernel,
        out_shape=wide_shapes(CACHE_SLOTS),
        in_specs=[vmem, anywhere],
        out_specs=(vmem, vmem),
        compiler_params=params,
        cost_estimate=cost(GROUP, CACHE_SLOTS),
        name="widen",
    )(kv, after)


def attend_local(first, heads, facts, q, keys, vals):
    return pl.pallas_call(
        functools.partial(local_kernel, first),
        out_shape=jax.ShapeDtypeStruct((heads, BLOCK_QUERIES, 2 * HEAD_SIZE), jnp.float32),
        in_specs=[vmem] * 4,
        out_specs=vmem,
        scratch_shapes=[pltpu.VMEM((2, STACK * BLOCK_QUERIES, CACHE_SLOTS), jnp.bfloat16)],
        compiler_params=params,
        cost_estimate=cost(GROUP, CACHE_SLOTS),
        name="attend_local",
    )(facts, q, keys, vals)


def attend_anchor(facts, moved, held, q, keys, vals, early, late):
    return pl.pallas_call(
        anchor_kernel,
        out_shape=jax.ShapeDtypeStruct(q.shape, jnp.bfloat16),
        in_specs=[vmem] * 8,
        out_specs=vmem,
        scratch_shapes=[
            pltpu.VMEM(held.shape, held.dtype),
            *(pltpu.VMEM(wide.shape, wide.dtype) for wide in wide_shapes(ANCHOR_SLOTS)),
            pltpu.VMEM((GROUP // STACK, STACK * BLOCK_QUERIES, ANCHOR_SLOTS), jnp.bfloat16),
            pltpu.VMEM((BLOCK_QUERIES, ANCHOR_SLOTS + CACHE_SLOTS), jnp.float32),
        ],
        compiler_params=params,
        cost_estimate=cost(GROUP, ANCHOR_SLOTS),
        name="attend_anchor",
    )(facts, moved, held, q, keys, vals, early, late)


def body(queries, kv_cache, anchor_src, stretch_pos):
    block = lax.axis_index("ctx").astype(jnp.int32)
    blocks = lax.axis_size("ctx")
    which = lax.broadcasted_iota(jnp.int32, (2, 8, 128), 0)
    facts = jnp.where(which == 0, stretch_pos.reshape(1, 1, 1) // TILE, block - anchor_src.reshape(1, 1, 1))
    held = lax.optimization_barrier(kv_cache[:, :ANCHOR_SLOTS, :])

    def from_earlier(held, shift):
        return lax.ppermute(held, "ctx", [(b, b + shift) for b in range(blocks - shift)])

    moved = from_earlier(held, 2)
    q = lax.all_to_all(cut(queries, held), "head", split_axis=0, concat_axis=0, tiled=True)
    q = q.reshape(BLOCK_QUERIES, GROUP * HEAD_SIZE)
    held = choose(2, facts, moved, held, facts, cost(GROUP, CACHE_SLOTS))
    moved = from_earlier(held, 1)
    keys, vals = widen(kv_cache, held)
    held = choose(1, facts, moved, held, keys, slight)
    early = attend_local(0, FIRST_HEADS, facts, q, keys, vals)
    held, early = lax.optimization_barrier((held, early))
    moved = from_earlier(held, 4)
    late = attend_local(FIRST_HEADS, GROUP - FIRST_HEADS, facts, q, keys, vals)
    result = attend_anchor(facts, moved, held, q, keys, vals, early, late)
    return lax.all_to_all(result, "head", split_axis=0, concat_axis=1, tiled=True)


def solution(mesh):
    in_specs = (P(("ctx", "head"), None), P(None, "ctx", "head"), P("ctx"), P("ctx"))
    out_specs = P(("ctx", "head"), None)
    return jax.shard_map(body, mesh=mesh, in_specs=in_specs, out_specs=out_specs, check_vma=False)
```
